256 devices in a mesh: dp: 16 (over y, z_hi), mp: 16 (over z_lo, x, core).
Axes of the slice: x: 4, y: 4, z: 8 (z_hi: 4, z_lo: 2; z = z_hi * 2 + z_lo), core: 2. Of those that a mesh axis runs over, the one named last changes fastest.
Arguments:
- dec_input: bfloat16 [16, 256, 4096], P('dp', None, 'mp'), may hold values from -6 to 6
- enc_output: bfloat16 [16, 256, 4096], P('dp', 'mp'), may hold values from -32 to 32
- query_weight: bfloat16 [4096, 4096], P('dp', 'mp'), may hold values from -3 to 3
- key_weight: bfloat16 [4096, 4096], P('dp', 'mp'), may hold values from -1 to 1
- value_weight: bfloat16 [4096, 4096], P('dp', 'mp'), may hold values from -0.09375 to 0.09375
- output_weight: bfloat16 [4096, 4096], P('mp', 'dp'), may hold values from -0.09375 to 0.09375
- cotangent: bfloat16 [16, 256, 4096], P('dp', None, 'mp'), may hold values from -6 to 6
- enc_lengths: int32 [16], P('dp'), may hold values from 64 to 256
- dec_lengths: int32 [16], P('dp'), may hold values from 64 to 256
Outputs:
- layer_out: bfloat16 [16, 256, 4096], P('dp', None, 'mp')
- input_grad: bfloat16 [16, 256, 4096], P('dp', None, 'mp')
- enc_grad: bfloat16 [16, 256, 4096], P('dp', 'mp')
- query_grad: bfloat16 [4096, 4096], P('dp', 'mp')
- key_grad: bfloat16 [4096, 4096], P('dp', 'mp')
- value_grad: bfloat16 [4096, 4096], P('dp', 'mp')
- output_grad: bfloat16 [4096, 4096], P('mp', 'dp')
The draws below stay inside these ranges and needn't reach their ends.
All inputs are finite; a program needn't handle non-finite values.
Results may differ from the reference program's by a relative error of at most 0.019.
The reference program's roundings to bfloat16 on the way (of `normed`, `probs_low`, `attended`, `masked`, `attended_grad` and `scores_grad`) count: a program that leaves them out, or rounds other values in their place, can miss the bound.
Values may be sent and summed in bfloat16 or wider, within the bound.
No kernel may reach another device: no remote copies, remote signals or barrier semaphores. Data moves between devices by JAX's collectives and lax.ppermute only.
A program may use at most 64 MiB of HBM per device.

```python
import jax
import jax.numpy as jnp
from jax import lax

D = 4096
H = 16
DH = 256
TGT = 256
LENC = 256
SEQS = 16
N_MP = 16


def common_weight(key):
    source = jax.random.fold_in(key, 202)
    return jnp.clip(jax.random.normal(source, (D, D), jnp.float32), -4.0, 4.0) * D ** (-0.5)


def draw_dec_input(key, part):
    key = jax.random.fold_in(key, 7)
    values = jnp.clip(jax.random.normal(key, (SEQS, TGT, D), jnp.float32), -6.0, 6.0)
    return values.astype(jnp.bfloat16)


def draw_enc_output(key, part):
    key = jax.random.fold_in(key, 11)
    values = jnp.clip(jax.random.normal(key, (SEQS, LENC, D), jnp.float32), -4.0, 4.0)
    return values.astype(jnp.bfloat16)


def draw_query_weight(key, part):
    key = jax.random.fold_in(key, 13)
    values = jnp.clip(jax.random.normal(key, (D, D), jnp.float32), -4.0, 4.0) * D ** (-0.5)
    return values.astype(jnp.bfloat16)


def draw_key_weight(key, part):
    return common_weight(key).astype(jnp.bfloat16)


def place_ends(values, rng, low, largest):
    index_at = [jax.random.randint(jax.random.fold_in(rng, axis), (), 0, length) for axis, length in enumerate(values.shape)]
    main_axis = values.shape.index(max(values.shape))
    beside = index_at[:main_axis] + [(index_at[main_axis] + 1) % values.shape[main_axis]] + index_at[main_axis + 1:]
    return values.at[tuple(index_at)].set(low).at[tuple(beside)].set(largest)


def levels(rng, dims, cuts, low, largest):
    gain, own = 1.0, jax.random.fold_in(rng, 6)
    for dim, parts in cuts:
        draws = jnp.exp(jax.random.uniform(jax.random.fold_in(own, dim), (parts,), jnp.float32, low / len(cuts), largest / len(cuts)))
        gain = gain * jnp.repeat(draws, dims[dim] // parts).reshape([-1 if axis == dim else 1 for axis in range(len(dims))])
    return gain


def scatter_about(stream_key, dims, scale, most, split=(), kind=jnp.bfloat16):
    array = scale * jax.random.normal(stream_key, dims, jnp.float32)
    if split:
        array = array * levels(stream_key, dims, split, -0.22, 0.18)
    return jnp.clip(array, -most, most).astype(kind)


def setup_inputs(seed: int = 0) -> dict:
    keys = jax.random.split(jax.random.key(seed), 10)
    return {
        "dec_input": draw_dec_input(jax.random.fold_in(keys[9], 71), 0),
        "enc_output": draw_enc_output(jax.random.fold_in(keys[9], 71), 0),
        "query_weight": draw_query_weight(jax.random.fold_in(keys[9], 71), 0),
        "key_weight": draw_key_weight(jax.random.fold_in(keys[9], 71), 0),
        "value_weight": scatter_about(keys[4], (D, D), D ** -0.5, 0.09375, ((0, 16), (1, 16))),
        "output_weight": scatter_about(keys[5], (D, D), D ** -0.5, 0.09375, ((0, 16), (1, 16))),
        "cotangent": scatter_about(keys[6], (SEQS, TGT, D), 1.0, 6.0, ((0, 16), (2, 16))),
        "enc_lengths": place_ends(jax.random.randint(keys[7], (SEQS,), LENC // 4, LENC + 1), jax.random.fold_in(keys[7], 1), LENC // 4, LENC).astype(jnp.int32),
        "dec_lengths": place_ends(jax.random.randint(keys[8], (SEQS,), TGT // 4, TGT + 1), jax.random.fold_in(keys[8], 1), TGT // 4, TGT).astype(jnp.int32),
    }


def round_sum(terms):
    rounded = lax.optimization_barrier(terms.astype(jnp.bfloat16))
    return lax.optimization_barrier(jnp.sum(rounded.astype(jnp.float32), axis=0))

def grouped(left, weight, groups):
    rows = left.shape[0]
    width = left.shape[1] // groups
    return jnp.einsum('rgk,gke->gre', left.reshape(rows, groups, width).astype(jnp.float32), weight.reshape(groups, width, weight.shape[1]).astype(jnp.float32))

def round_once(term):
    return lax.optimization_barrier(term.astype(jnp.bfloat16)).astype(jnp.float32)

def reference(dec_input, enc_output, query_weight, key_weight, value_weight, output_weight, cotangent, enc_lengths, dec_lengths):
    scale = DH ** (-0.5)

    def one_seq(totals, inputs):
        hidden, encoded, upstream, enc_len, dec_len = inputs
        hidden32 = hidden.astype(jnp.float32)
        inv_rms = lax.rsqrt(lax.optimization_barrier(jnp.mean(hidden32 * hidden32, axis=-1, keepdims=True)) + 1e-06)
        normed = (hidden32 * inv_rms).astype(jnp.bfloat16)
        query = jnp.dot(normed, query_weight, preferred_element_type=jnp.float32).astype(jnp.bfloat16)
        keyed = jnp.dot(encoded, key_weight, preferred_element_type=jnp.float32).astype(jnp.bfloat16)
        valued = jnp.dot(encoded, value_weight, preferred_element_type=jnp.float32).astype(jnp.bfloat16)
        query_heads = query.reshape(TGT, H, DH).astype(jnp.float32)
        key_heads = keyed.reshape(LENC, H, DH).astype(jnp.float32)
        value_heads = valued.reshape(LENC, H, DH).astype(jnp.float32)
        scores = jnp.einsum('thd,lhd->htl', query_heads, key_heads) * scale
        valid = jnp.arange(LENC, dtype=jnp.int32) < enc_len
        scores = jnp.where(valid[None, None, :], scores, -1e+30)
        shifted = jnp.exp(scores - lax.optimization_barrier(jnp.max(scores, axis=-1, keepdims=True)))
        probs = shifted / lax.optimization_barrier(jnp.sum(shifted, axis=-1, keepdims=True))
        probs_low = probs.astype(jnp.bfloat16)
        attended = jnp.einsum('htl,lhd->thd', probs_low.astype(jnp.float32), value_heads).reshape(TGT, D).astype(jnp.bfloat16)
        attn_out = round_sum(grouped(attended, output_weight, N_MP))
        layer_out = (hidden32 + attn_out).astype(jnp.bfloat16)
        keep = (jnp.arange(TGT, dtype=jnp.int32) < dec_len)[:, None]
        masked = jnp.where(keep, upstream, jnp.zeros_like(upstream))
        attended_grad = jnp.dot(masked, output_weight.T, preferred_element_type=jnp.float32).astype(jnp.bfloat16)
        grad_heads = attended_grad.reshape(TGT, H, DH).astype(jnp.float32)
        probs_grad = jnp.einsum('thd,lhd->htl', grad_heads, value_heads)
        scores_grad = (probs * (probs_grad - lax.optimization_barrier(jnp.sum(probs * probs_grad, axis=-1, keepdims=True))) * scale).astype(jnp.bfloat16)
        scores_grad32 = scores_grad.astype(jnp.float32)
        q_grad = jnp.einsum('htl,lhd->thd', scores_grad32, key_heads).reshape(TGT, D).astype(jnp.bfloat16)
        k_grad = jnp.einsum('htl,thd->lhd', scores_grad32, query_heads).reshape(LENC, D).astype(jnp.bfloat16)
        v_grad = jnp.einsum('htl,thd->lhd', probs_low.astype(jnp.float32), grad_heads).reshape(LENC, D).astype(jnp.bfloat16)
        normed_grad = round_sum(grouped(q_grad, query_weight.T, N_MP))
        stat = lax.optimization_barrier(jnp.mean(normed_grad * hidden32, axis=-1, keepdims=True))
        input_grad = (masked.astype(jnp.float32) + inv_rms * normed_grad - hidden32 * inv_rms ** 3 * stat).astype(jnp.bfloat16)
        enc_terms = grouped(k_grad, key_weight.T, N_MP) + grouped(v_grad, value_weight.T, N_MP)
        enc_grad = round_sum(enc_terms).astype(jnp.bfloat16)
        query_term = round_once(jnp.dot(normed.T, q_grad, preferred_element_type=jnp.float32))
        key_term = round_once(jnp.dot(encoded.T, k_grad, preferred_element_type=jnp.float32))
        value_term = round_once(jnp.dot(encoded.T, v_grad, preferred_element_type=jnp.float32))
        output_term = round_once(jnp.dot(attended.T, masked, preferred_element_type=jnp.float32))
        totals = (totals[0] + query_term, totals[1] + key_term, totals[2] + value_term, totals[3] + output_term)
        return (totals, (layer_out, input_grad, enc_grad))
    zeros = jnp.zeros((D, D), jnp.float32)
    totals, stacked = lax.scan(one_seq, (zeros, zeros, zeros, zeros), (dec_input, enc_output, cotangent, enc_lengths, dec_lengths))
    return (stacked[0], stacked[1], stacked[2], totals[0].astype(jnp.bfloat16), totals[1].astype(jnp.bfloat16), totals[2].astype(jnp.bfloat16), totals[3].astype(jnp.bfloat16))
```

```python
import functools

import jax
import jax.numpy as jnp
from jax import lax
from jax.experimental import pallas as pl
from jax.experimental.pallas import tpu as pltpu
from jax.sharding import PartitionSpec as P

BF = jnp.bfloat16
F32 = jnp.float32
NB = 16
VMEM = 40 * 1024 * 1024

ZXC = [(a, b, c) for a in range(2) for b in range(4) for c in range(2)]


def mp_index(a, b, c):
    return (a % 2) * 8 + (b % 4) * 2 + (c % 2)


def mp_shift(da, db, dc):
    return [(mp_index(a, b, c), mp_index(a + da, b + db, c + dc)) for a, b, c in ZXC]


def nn(a, b):
    return lax.dot_general(a, b, (((1,), (0,)), ((), ())), preferred_element_type=F32)


def nt(a, b):
    return lax.dot_general(a, b, (((1,), (1,)), ((), ())), preferred_element_type=F32)


def tn(a, b):
    return lax.dot_general(a, b, (((0,), (0,)), ((), ())), preferred_element_type=F32)


def attention(scale, enc_len, query, keyed, valued, attended_grad):
    scores = nt(query, keyed) * scale
    column = lax.broadcasted_iota(jnp.int32, scores.shape, 1)
    scores = jnp.where(column < enc_len, scores, -1e30)
    shifted = jnp.exp(scores - jnp.max(scores, axis=-1, keepdims=True))
    probs = shifted / jnp.sum(shifted, axis=-1, keepdims=True)
    probs_low = probs.astype(BF)
    attended = nn(probs_low, valued).astype(BF)
    probs_grad = nt(attended_grad, valued)
    inner = jnp.sum(probs * probs_grad, axis=-1, keepdims=True)
    scores_grad = (probs * (probs_grad - inner) * scale).astype(BF)
    q_grad = nn(scores_grad, keyed).astype(BF)
    k_grad = tn(scores_grad, query).astype(BF)
    v_grad = tn(probs_low, attended_grad).astype(BF)
    stat = jnp.sum(q_grad.astype(F32) * query.astype(F32), axis=-1, keepdims=True)
    return q_grad, k_grad, v_grad, attended, stat


def forward_kernel(
    scale, length_ref, normed_ref, masked_ref, enc_ref, weight_ref,
    qg_ref, kg_ref, vg_ref, at_ref, stat_ref, q_acc, kv_acc, g_acc,
):
    step = pl.program_id(0)
    width = q_acc.shape[1]

    @pl.when(step == 0)
    def _():
        q_acc[...] = jnp.zeros_like(q_acc)
        kv_acc[...] = jnp.zeros_like(kv_acc)
        g_acc[...] = jnp.zeros_like(g_acc)

    q_acc[...] += nn(normed_ref[0], weight_ref[:, :width])
    kv_acc[...] += nn(enc_ref[0], weight_ref[:, width : 3 * width])
    g_acc[...] += nn(masked_ref[0], weight_ref[:, 3 * width :])

    @pl.when(step == pl.num_programs(0) - 1)
    def _():
        query = q_acc[...].astype(BF)
        keyed = kv_acc[:, :width].astype(BF)
        valued = kv_acc[:, width:].astype(BF)
        out = attention(scale, length_ref[0], query, keyed, valued, g_acc[...].astype(BF))
        qg_ref[...], kg_ref[...], vg_ref[...], at_ref[...] = out[:4]
        stat_ref[...] = jnp.broadcast_to(out[4], stat_ref.shape)


def weight_grad_kernel(normed_ref, masked_ref, enc_ref, qg_ref, kg_ref, vg_ref, at_ref, out_ref):
    width = qg_ref.shape[1]
    out_ref[:, :width] = tn(normed_ref[0], qg_ref[...]).astype(BF)
    out_ref[:, width : 2 * width] = tn(enc_ref[0], kg_ref[...]).astype(BF)
    out_ref[:, 2 * width : 3 * width] = tn(enc_ref[0], vg_ref[...]).astype(BF)
    out_ref[:, 3 * width :] = tn(masked_ref[0], at_ref[...]).astype(BF)


def partial_kernel(weight_ref, qg_ref, kg_ref, vg_ref, at_ref, out_ref):
    step = pl.program_id(0)
    width = qg_ref.shape[1]
    a, b, c = step // 8, (step // 2) % 4, step % 2
    out_ref[c, b, a, 0] = nt(qg_ref[...], weight_ref[:, :width]).astype(BF)
    out_ref[c, b, a, 1] = nt(at_ref[...], weight_ref[:, 3 * width :]).astype(BF)
    enc = nt(kg_ref[...], weight_ref[:, width : 2 * width])
    enc += nt(vg_ref[...], weight_ref[:, 2 * width : 3 * width])
    enc = enc.astype(BF)
    rows = enc.shape[0] // NB
    start = pl.multiple_of(step * rows, rows)
    for n, (a, b, c) in enumerate(ZXC):
        out_ref[c, b, a, 2, pl.ds(start, rows), :] = enc[n * rows : (n + 1) * rows]


def call(kernel, grid, ins, outs, scratch, args, flops):
    return pl.pallas_call(
        kernel,
        grid=(grid,),
        in_specs=ins,
        out_specs=[s for s, _ in outs],
        out_shape=[o for _, o in outs],
        scratch_shapes=scratch,
        compiler_params=pltpu.CompilerParams(
            dimension_semantics=("arbitrary",), vmem_limit_bytes=VMEM
        ),
        cost_estimate=pl.CostEstimate(flops=flops, bytes_accessed=16 << 20, transcendentals=0),
    )(*args)


def gather_mp(acts, a, b, c):
    other = lax.ppermute(acts, "mp", mp_shift(1, 0, 0))
    pair = jnp.where(a == 0, jnp.stack([acts, other]), jnp.stack([other, acts]))
    line = jnp.zeros((4,) + pair.shape, pair.dtype)
    parts = [pair] + [lax.ppermute(pair, "mp", mp_shift(0, d, 0)) for d in (1, 2, 3)]
    for d, part in enumerate(parts):
        line = lax.dynamic_update_index_in_dim(line, part, (b - d) % 4, 0)
    sibling = lax.ppermute(line, "mp", mp_shift(0, 0, 1))
    return jnp.where(c == 0, jnp.stack([line, sibling]), jnp.stack([sibling, line]))


def take(array, index):
    return lax.dynamic_index_in_dim(array, index, 0, keepdims=False)


def scatter_mp(parts, a, b, c):
    got = lax.ppermute(take(parts, 1 - c), "mp", mp_shift(0, 0, 1))
    line = (take(parts, c).astype(F32) + got.astype(F32)).astype(BF)
    total = take(line, b).astype(F32)
    for d in (1, 2, 3):
        got = lax.ppermute(take(line, (b + d) % 4), "mp", mp_shift(0, d, 0))
        total = total + got.astype(F32)
    pair = total.astype(BF)
    got = lax.ppermute(take(pair, 1 - a), "mp", mp_shift(1, 0, 0))
    return take(pair, a).astype(F32) + got.astype(F32)


def sum_mp(value):
    for shift in ((0, 0, 1), (0, 2, 0), (1, 0, 0)):
        value = value + lax.ppermute(value, "mp", mp_shift(*shift))
    flip = [(mp_index(a, b, c), mp_index(a, b ^ 1, c)) for a, b, c in ZXC]
    return value + lax.ppermute(value, "mp", flip)


def local(
    dec_input,
    enc_output,
    query_weight,
    key_weight,
    value_weight,
    output_weight,
    cotangent,
    enc_lengths,
    dec_lengths,
):
    place = lax.axis_index("mp")
    a, b, c = place // 8, (place // 2) % 4, place % 2
    tokens, feat = dec_input.shape[1:]
    width = query_weight.shape[1]
    erows = enc_output.shape[1]
    keys = erows * NB
    scale = width ** (-0.5)

    weights = lax.all_gather(
        jnp.concatenate([query_weight, key_weight, value_weight, output_weight.T], axis=1),
        "dp", axis=0, tiled=True,
    )

    own_enc = enc_output[0].reshape(erows, NB, feat).transpose(1, 0, 2).reshape(NB * erows, feat)
    acts = gather_mp(jnp.stack([dec_input[0], cotangent[0], own_enc]), a, b, c)
    acts = acts.transpose(2, 1, 0, 3, 4, 5).reshape(NB, 3, tokens, feat)
    hidden32 = acts[:, 0].astype(F32)
    square = jnp.sum(hidden32 * hidden32, axis=(0, 2))[:, None] / (NB * feat)
    inv_rms = lax.rsqrt(square + 1e-06)
    normed = (hidden32 * inv_rms).astype(BF)
    keep = (jnp.arange(tokens, dtype=jnp.int32) < dec_lengths[0])[:, None]
    masked = jnp.where(keep, acts[:, 1], jnp.zeros((), BF))
    encoded = (
        acts[:, 2].reshape(NB, NB, erows, feat).transpose(1, 0, 2, 3).reshape(NB, keys, feat)
    )

    block = pl.BlockSpec((1, tokens, feat), lambda i: (i, 0, 0))
    eblock = pl.BlockSpec((1, keys, feat), lambda i: (i, 0, 0))
    wblock = pl.BlockSpec((feat, 4 * width), lambda i: (i, 0))
    tspec = pl.BlockSpec((tokens, width), lambda i: (0, 0))
    kspec = pl.BlockSpec((keys, width), lambda i: (0, 0))
    tshape = jax.ShapeDtypeStruct((tokens, width), BF)
    kshape = jax.ShapeDtypeStruct((keys, width), BF)
    unit = 2 * tokens * feat * width * NB
    q_grad, k_grad, v_grad, attended, stat = call(
        functools.partial(forward_kernel, scale),
        NB,
        [pl.BlockSpec(memory_space=pltpu.SMEM), block, block, eblock, wblock],
        [
            (tspec, tshape), (kspec, kshape), (kspec, kshape), (tspec, tshape),
            (pl.BlockSpec((tokens, 128), lambda i: (0, 0)),
             jax.ShapeDtypeStruct((tokens, 128), F32)),
        ],
        [
            pltpu.VMEM((tokens, width), F32),
            pltpu.VMEM((keys, 2 * width), F32),
            pltpu.VMEM((tokens, width), F32),
        ],
        (enc_lengths, normed, masked, encoded, weights),
        4 * unit,
    )
    (grads,) = call(
        weight_grad_kernel,
        NB,
        [block, block, eblock, tspec, kspec, kspec, tspec],
        [(wblock, jax.ShapeDtypeStruct((NB * feat, 4 * width), BF))],
        [],
        (normed, masked, encoded, q_grad, k_grad, v_grad, attended),
        4 * unit,
    )
    share = lax.psum_scatter(grads, "dp", scatter_dimension=0, tiled=True)
    (parts,) = call(
        partial_kernel,
        NB,
        [wblock, tspec, kspec, kspec, tspec],
        [(
            pl.BlockSpec((2, 4, 2, 3, tokens, feat), lambda i: (0,) * 6),
            jax.ShapeDtypeStruct((2, 4, 2, 3, tokens, feat), BF),
        )],
        [],
        (weights, q_grad, k_grad, v_grad, attended),
        4 * unit,
    )
    stat = sum_mp(stat[:, :1]) / (NB * feat)
    total = scatter_mp(parts, a, b, c)

    own = dec_input[0].astype(F32)
    own_masked = jnp.where(keep, cotangent[0], jnp.zeros((), BF)).astype(F32)
    layer_out = (own + total[1]).astype(BF)[None]
    input_grad = (own_masked + inv_rms * total[0] - own * (inv_rms * inv_rms * stat)).astype(BF)[None]
    enc_grad = (
        total[2].astype(BF).reshape(NB, erows, feat).transpose(1, 0, 2).reshape(1, erows, NB * feat)
    )
    query_grad = share[:, :width]
    key_grad = share[:, width : 2 * width]
    value_grad = share[:, 2 * width : 3 * width]
    output_grad = share[:, 3 * width :].T
    return (layer_out, input_grad, enc_grad, query_grad, key_grad, value_grad, output_grad)


def solution(mesh):
    in_specs = (
        P("dp", None, "mp"),
        P("dp", "mp", None),
        P("dp", "mp"),
        P("dp", "mp"),
        P("dp", "mp"),
        P("mp", "dp"),
        P("dp", None, "mp"),
        P("dp"),
        P("dp"),
    )
    out_specs = (
        P("dp", None, "mp"),
        P("dp", None, "mp"),
        P("dp", "mp", None),
        P("dp", "mp"),
        P("dp", "mp"),
        P("dp", "mp"),
        P("mp", "dp"),
    )
    return jax.shard_map(local, mesh=mesh, in_specs=in_specs, out_specs=out_specs, check_vma=False)
```

```python
import functools

import jax
import jax.numpy as jnp
from jax import lax
from jax.experimental import pallas as pl
from jax.experimental.pallas import tpu as pltpu
from jax.sharding import PartitionSpec as P

BF = jnp.bfloat16
F32 = jnp.float32
NB = 16
MIB = 1024 * 1024
COST = 16
EXTRA = 16

YZ = [(y, z) for y in range(4) for z in range(4)]
ZXC = [(a, b, c) for a in range(2) for b in range(4) for c in range(2)]


def dp_index(y, z):
    return (y % 4) * 4 + (z % 4)


def mp_index(a, b, c):
    return (a % 2) * 8 + (b % 4) * 2 + (c % 2)


def send_y(value, d):
    return lax.ppermute(value, "dp", [(dp_index(y, z), dp_index(y + d, z)) for y, z in YZ])


def send_z(value, d):
    return lax.ppermute(value, "dp", [(dp_index(y, z), dp_index(y, z + d)) for y, z in YZ])


def send_mp(value, da, db, dc):
    pairs = [(mp_index(a, b, c), mp_index(a + da, b + db, c + dc)) for a, b, c in ZXC]
    return lax.ppermute(value, "mp", pairs)


def send_x(value, bits):
    pairs = [(mp_index(a, b, c), mp_index(a, b ^ bits, c)) for a, b, c in ZXC]
    return lax.ppermute(value, "mp", pairs)


def nn(a, b):
    return lax.dot_general(a, b, (((1,), (0,)), ((), ())), preferred_element_type=F32)


def nt(a, b):
    return lax.dot_general(a, b, (((1,), (1,)), ((), ())), preferred_element_type=F32)


def tn(a, b):
    return lax.dot_general(a, b, (((0,), (0,)), ((), ())), preferred_element_type=F32)


def shape_of(shape, dtype=BF):
    return jax.ShapeDtypeStruct(shape, dtype)


def call(kernel, args, outs, scalars=(), scratch=(), flops=0, moved=0, vmem=8):
    spec = pl.BlockSpec(memory_space=pltpu.VMEM)
    return pl.pallas_call(
        kernel,
        in_specs=[pl.BlockSpec(memory_space=pltpu.SMEM)] * len(scalars) + [spec] * len(args),
        out_specs=[spec] * len(outs),
        out_shape=outs,
        scratch_shapes=scratch,
        compiler_params=pltpu.CompilerParams(vmem_limit_bytes=vmem * MIB),
        cost_estimate=pl.CostEstimate(flops=COST * flops, bytes_accessed=moved, transcendentals=0),
    )(*scalars, *args)


def call_out(kernel, args, outs, scalars=()):
    spec = pl.BlockSpec(memory_space=pltpu.VMEM)
    n = len(outs)

    def body(*refs):
        ins, results, sems = refs[: -2 * n - 1], refs[-2 * n - 1 : -n - 1], refs[-1]
        held = refs[-n - 1 : -1]
        kernel(*ins, *held)
        copies = [
            pltpu.make_async_copy(a, b, sems.at[k]) for k, (a, b) in enumerate(zip(held, results))
        ]
        for copy in copies:
            copy.start()
        for copy in copies:
            copy.wait()

    return pl.pallas_call(
        body,
        in_specs=[pl.BlockSpec(memory_space=pltpu.SMEM)] * len(scalars) + [spec] * len(args),
        out_specs=[pl.BlockSpec(memory_space=pltpu.HBM)] * n,
        out_shape=outs,
        scratch_shapes=[pltpu.VMEM(o.shape, o.dtype) for o in outs] + [pltpu.SemaphoreType.DMA((n,))],
        compiler_params=pltpu.CompilerParams(vmem_limit_bytes=8 * MIB),
    )(*scalars, *args)


def mp_place():
    place = lax.axis_index("mp")
    return lax.div(place, 8), lax.rem(lax.div(place, 2), 4), lax.rem(place, 2)


def dp_block(dy, dz):
    part = lax.axis_index("dp")
    return lax.rem(lax.div(part, 4) + dy, 4) * 4 + lax.rem(lax.rem(part, 4) + dz, 4)


def blocks_at(dz):
    return [dp_block(dy, dz) for dy in range(4)]


def after(values, *others):
    out = lax.optimization_barrier((others, tuple(values)))
    return out[1]


def pack_stat(row, shape):
    high = row.astype(BF).astype(F32)
    line = lax.broadcasted_iota(jnp.int32, shape, 0)
    rows = jnp.where(line == 0, high, jnp.where(line == 1, row - high, 0.0))
    return rows.astype(BF)


def stat_of(rows):
    return jnp.sum(rows.astype(F32), axis=0, keepdims=True)


def assemble_kernel(q_ref, k_ref, v_ref, o_ref, dec_ref, cot_ref, enc_ref, block_ref, acts_ref, o_buf, enc_buf, sems):
    width, feat = q_ref.shape[1], cot_ref.shape[2]
    tokens, erows = cot_ref.shape[1], enc_ref.shape[1]
    pairs = [(ref, block_ref.at[:, n * width : (n + 1) * width]) for n, ref in enumerate((q_ref, k_ref, v_ref))]
    pairs += [(o_ref, o_buf), (enc_ref.at[0], enc_buf)]
    pairs += [(dec_ref.at[0], acts_ref.at[:tokens]), (cot_ref.at[0], acts_ref.at[tokens : 2 * tokens])]
    copies = [pltpu.make_async_copy(a, b, sems.at[n]) for n, (a, b) in enumerate(pairs)]
    for copy in copies:
        copy.start()
    copies[3].wait()
    block_ref[:, 3 * width :] = o_buf[...].T
    copies[4].wait()
    for n in range(NB):
        line = 2 * tokens + n * erows
        acts_ref[line : line + erows] = enc_buf[:, n * feat : (n + 1) * feat]
    for n in (0, 1, 2, 5, 6):
        copies[n].wait()


def pair_kernel(first, second, out_ref):
    out_ref[0] = first[...]
    out_ref[1] = second[...]


def pick_kernel(first, second, out_first, out_second):
    out_first[...] = first[0]
    out_second[...] = second[1]


def halves_kernel(first, second, out_first, out_second):
    half = out_first.shape[0]
    out_first[...] = first[:half]
    out_second[...] = second[half:]


def prepare_kernel(len_ref, *refs):
    pieces, (normed_ref, masked_ref, enc_ref, inv_ref) = refs[:4], refs[4:]
    tokens, feat = normed_ref.shape[1:]
    erows = enc_ref.shape[1] // NB
    a, b, c = mp_place()
    square = jnp.zeros((tokens, 1), F32)
    for piece in pieces:

        def add_squares(k, total, piece=piece):
            hidden = piece[lax.div(k, 2), lax.rem(k, 2), :tokens].astype(F32)
            return total + jnp.sum(hidden * hidden, axis=1, keepdims=True)

        square = lax.fori_loop(0, 4, add_squares, square)
    inv_rms = lax.rsqrt(square / (NB * feat) + 1e-06)
    inv_ref[...] = jnp.broadcast_to(inv_rms, inv_ref.shape)
    keep = lax.broadcasted_iota(jnp.int32, (tokens, feat), 0) < len_ref[0]
    for n, piece in enumerate(pieces):

        def write(k, carry, n=n, piece=piece):
            x, z = lax.div(k, 2), lax.rem(k, 2)
            spot = lax.bitwise_xor(b, x + 2 * (n % 2))
            place = lax.rem(a + z, 2) * 8 + spot * 2 + lax.rem(c + n // 2, 2)
            normed_ref[place] = (piece[x, z, :tokens].astype(F32) * inv_ref[:, :1]).astype(BF)
            rows = piece[x, z, tokens : 2 * tokens]
            masked_ref[place] = jnp.where(keep, rows.astype(F32), 0.0).astype(BF)
            start = pl.multiple_of(place * erows, erows)
            for m in range(NB):
                line = 2 * tokens + m * erows
                enc_ref[m, pl.ds(start, erows), :] = piece[x, z, line : line + erows]
            return carry

        lax.fori_loop(0, 4, write, 0)


def attention(scale, enc_len, query, keyed, valued, attended_grad):
    scores = nt(query, keyed) * scale
    column = lax.broadcasted_iota(jnp.int32, scores.shape, 1)
    scores = jnp.where(column < enc_len, scores, -1e30)
    shifted = jnp.exp(scores - jnp.max(scores, axis=-1, keepdims=True))
    probs = shifted / jnp.sum(shifted, axis=-1, keepdims=True)
    probs_low = probs.astype(BF)
    attended = nn(probs_low, valued).astype(BF)
    probs_grad = nt(attended_grad, valued)
    inner = jnp.sum(probs * probs_grad, axis=-1, keepdims=True)
    scores_grad = (probs * (probs_grad - inner) * scale).astype(BF)
    q_grad = nn(scores_grad, keyed).astype(BF)
    k_grad = tn(scores_grad, query).astype(BF)
    v_grad = tn(probs_low, attended_grad).astype(BF)
    stat = jnp.sum(q_grad.astype(F32) * query.astype(F32), axis=-1, keepdims=True)
    return q_grad, k_grad, v_grad, attended, stat


def project(places, pieces, normed_ref, masked_ref, enc_ref, stack_ref, init):
    width = stack_ref.shape[2] // 4
    for n, piece in enumerate(pieces):
        stack_ref[n] = piece()
    out = init
    for n in range(0, len(pieces), 4):
        group = places[n : n + 4]
        rows = jnp.concatenate([stack_ref[n + k] for k in range(4)], axis=0)
        normed, enc, masked = (
            jnp.concatenate([ref[p] for p in group], axis=1)
            for ref in (normed_ref, enc_ref, masked_ref)
        )
        new = (
            nn(normed, rows[:, :width]),
            nn(enc, rows[:, width : 2 * width]),
            nn(enc, rows[:, 2 * width : 3 * width]),
            nn(masked, rows[:, 3 * width :]),
        )
        out = new if out is None else tuple(o + v for o, v in zip(out, new))
    return out


def one(ref):
    return lambda: ref[...]


def at(ref, n):
    return lambda: ref[n]


def both(low, high):
    return lambda: jnp.concatenate([low[...], high[...]], axis=0)


def own_kernel(normed_ref, masked_ref, enc_ref, *refs):
    own, high, low, across, acc_ref, stack_ref = refs
    pieces = [one(own), one(high), one(across), one(low)]
    acc = project(blocks_at(0), pieces, normed_ref, masked_ref, enc_ref, stack_ref, None)
    for n in range(4):
        acc_ref[n] = acc[n]


def near_kernel(normed_ref, masked_ref, enc_ref, *refs):
    pair, high, low, across_b, across_a, acc_in, acc_ref, stack_ref = refs
    pieces = [at(pair, 0), at(high, 0), one(across_b), at(low, 0)]
    pieces += [at(pair, 1), at(high, 1), one(across_a), at(low, 1)]
    places = blocks_at(3) + blocks_at(1)
    init = [acc_in[n] for n in range(4)]
    acc = project(places, pieces, normed_ref, masked_ref, enc_ref, stack_ref, init)
    for n in range(4):
        acc_ref[n] = acc[n]


def far_kernel(scale, len_ref, normed_ref, masked_ref, enc_ref, *refs):
    far, high, low, across_low, across_high, acc_in = refs[:6]
    qg_ref, kv_ref, at_ref, qgt_ref, kvt_ref, att_ref, stat_ref, stack_ref = refs[6:]
    pieces = [one(far), one(high), both(across_low, across_high), one(low)]
    init = [acc_in[n] for n in range(4)]
    acc = project(blocks_at(2), pieces, normed_ref, masked_ref, enc_ref, stack_ref, init)
    out = attention(scale, len_ref[0], *(value.astype(BF) for value in acc))
    q_grad, k_grad, v_grad, attended, stat = out
    width = q_grad.shape[1]
    qg_ref[...] = q_grad
    kv_ref[:, :width] = k_grad
    kv_ref[:, width:] = v_grad
    at_ref[...] = attended
    qgt_ref[...] = q_grad.T
    kvt_ref[:width] = k_grad.T
    kvt_ref[width:] = v_grad.T
    att_ref[...] = attended.T
    row = jnp.broadcast_to(stat, (stat.shape[0], 128)).T[0:1]
    stat_ref[...] = pack_stat(row, stat_ref.shape)


def weight_grad_kernel(dz, normed_ref, masked_ref, enc_ref, *refs):
    qgt_ref, kvt_ref, att_ref = refs[:3]
    outs = list(refs[3:])
    width = qgt_ref.shape[0]
    for n in range(4):
        place = dp_block(n, dz)
        query = nn(qgt_ref[...], normed_ref[place]).astype(BF)
        pair = nn(kvt_ref[...], enc_ref[place]).astype(BF)
        attn = nn(att_ref[...], masked_ref[place]).astype(BF)
        if n == 2 and len(outs) == 3:
            low, high = outs.pop(0), outs.pop(0)
            low[:width] = query
            low[width:] = pair[:width]
            high[:width] = pair[width:]
            high[width:] = attn
        else:
            out = outs.pop(0)
            out[:width] = query
            out[width : 3 * width] = pair
            out[3 * width :] = attn


def partial_kernel(qg_ref, kv_ref, at_ref, stat_ref, *refs):
    stacks, outs, enc_buf = refs[:3], refs[3:5], refs[5]
    tokens, width = qg_ref.shape
    keys, feat = enc_buf.shape
    erows = keys // NB
    a, b, c = mp_place()
    for out in outs:
        for xr in range(4):
            for zr in range(2):
                out[xr, zr, 3 * tokens :, :] = stat_ref[...]
    for stack, shifts in zip(stacks, ((0, 0), (3, 1), (2, 2))):

        def body(n, carry, stack=stack, shifts=shifts):
            place = dp_block(lax.rem(n, 4), jnp.where(n < 4, shifts[0], shifts[1]))
            weight = stack[n]
            norm_part = nt(qg_ref[...], weight[:, :width]).astype(BF)
            out_part = nt(at_ref[...], weight[:, 3 * width :]).astype(BF)
            enc_buf[...] = nt(kv_ref[...], weight[:, width : 3 * width]).astype(BF)
            xr = lax.bitwise_xor(lax.rem(lax.div(place, 2), 4), b)
            zr = lax.rem(lax.div(place, 8) + 2 - a, 2)
            cr = lax.rem(lax.rem(place, 2) + 2 - c, 2)
            line = pl.multiple_of(2 * tokens + place * erows, erows)
            for k, out in enumerate(outs):

                @pl.when(cr == k)
                def _():
                    out[xr, zr, :tokens, :] = norm_part
                    out[xr, zr, tokens : 2 * tokens, :] = out_part

                for x in range(4):
                    for z in range(2):
                        owner = lax.rem(a + z, 2) * 8 + lax.bitwise_xor(b, x) * 2 + lax.rem(c + k, 2)
                        start = pl.multiple_of(owner * erows, erows)
                        out[x, z, pl.ds(line, erows), :] = enc_buf[pl.ds(start, erows), :]
            return carry

        lax.fori_loop(0, stack.shape[0], body, 0, unroll=2)


def add_rows(ins, out):
    rows, feat = out.shape[0] - EXTRA, out.shape[1]

    def body(step, carry):
        part = pl.ds(pl.multiple_of(step * CHUNK, CHUNK), CHUNK)
        total = ins[0][part, :].astype(F32)
        for ref in ins[1:]:
            total += ref[part, :].astype(F32)
        out[part, :] = total.astype(BF)
        return carry

    lax.fori_loop(0, rows // CHUNK, body, 0)
    stat = stat_of(ins[0][rows:])
    for ref in ins[1:]:
        stat += stat_of(ref[rows:])
    out[rows:] = pack_stat(stat, (EXTRA, feat))


def core_sum_kernel(keep_ref, got_ref, near_ref, far_ref):
    for x, out in enumerate((near_ref.at[0], near_ref.at[1], far_ref.at[0], far_ref.at[1])):
        for z in range(2):
            add_rows([keep_ref.at[x, z], got_ref.at[x, z]], out.at[z])


def split_sum_kernel(first_ref, second_ref, *outs):
    for n, out in enumerate(outs):
        if len(out.shape) == 2:
            add_rows([first_ref.at[n], second_ref.at[n]], out)
        else:
            for z in range(2):
                add_rows([first_ref.at[n, z], second_ref.at[n, z]], out.at[z])


def share_kernel(*refs):
    ins, outs = refs[:-4], refs[-4:]
    total = ins[0][...].astype(F32)
    for ref in ins[1:]:
        total += ref[...].astype(F32)
    total = total.astype(BF)
    width = outs[0].shape[1]
    for n, out in enumerate(outs[:3]):
        out[...] = total[n * width : (n + 1) * width].T
    outs[3][...] = total[3 * width :]


def last_kernel(len_ref, own_ref, got_ref, acts_ref, inv_ref, out_ref, in_ref, enc_ref):
    tokens, feat = out_ref.shape[1:]
    rows = 3 * tokens
    stat = stat_of(own_ref[rows:]) + stat_of(got_ref[rows:])
    stat = jnp.broadcast_to(stat, (128, tokens)).T[:, :1] / (NB * feat)
    total = [
        own_ref[n * tokens : (n + 1) * tokens].astype(F32)
        + got_ref[n * tokens : (n + 1) * tokens].astype(F32)
        for n in range(3)
    ]
    inv_rms = inv_ref[:, :1]
    dec = acts_ref[:tokens].astype(F32)
    out_ref[0] = (dec + total[1]).astype(BF)
    keep = lax.broadcasted_iota(jnp.int32, (tokens, feat), 0) < len_ref[0]
    masked = jnp.where(keep, acts_ref[tokens : 2 * tokens].astype(F32), 0.0)
    in_grad = masked + inv_rms * total[0] - dec * (inv_rms * inv_rms * stat)
    in_ref[0] = in_grad.astype(BF)
    erows = enc_ref.shape[1]
    for n in range(NB):
        enc_ref[0, :, n * feat : (n + 1) * feat] = total[2][n * erows : (n + 1) * erows].astype(BF)


def stack_pair(first, second):
    return call(pair_kernel, (first, second), [shape_of((2,) + first.shape)])[0]


def gather(block, acts):
    before, behind = send_z(block, 1), send_z(block, -1)
    low, high = send_y(block, 1), send_y(block, -1)
    other = send_mp(acts, 1, 0, 0)
    other, again = after((other, block), low, high)
    pair_acts = stack_pair(acts, other)
    next_acts = send_x(pair_acts, 1)
    across = send_y(again, 2)

    pair_acts, next_acts, far, before, behind = after(
        (pair_acts, next_acts, block, before, behind), across
    )
    quad = stack_pair(pair_acts, next_acts)
    far_quad = send_x(quad, 2)
    pair = stack_pair(before, behind)
    pair_low, pair_high = send_y(pair, 1), send_y(pair, -1)
    far = send_z(far, 2)

    pair_low, pair_high, far = after((pair_low, pair_high, far))
    to_low, to_high = call(pick_kernel, (pair_low, pair_high), [shape_of(block.shape)] * 2)
    across_b, across_a = send_y(to_low, 1), send_y(to_high, -1)
    f_low, f_high = send_y(far, 1), send_y(far, -1)

    quad, far_quad, f_low, f_high = after((quad, far_quad, f_low, f_high), across_a, across_b)
    pieces = [quad, far_quad, send_mp(quad, 0, 0, 1), send_mp(far_quad, 0, 0, 1)]
    half = shape_of((block.shape[0] // 2, block.shape[1]))
    to_low, to_high = call(halves_kernel, (f_low, f_high), [half] * 2)
    last_low, last_high = send_y(to_low, 1), send_y(to_high, -1)
    return (
        (block, high, low, across),
        (pair, pair_high, pair_low, across_b, across_a),
        (far, f_high, f_low, last_low, last_high),
        pieces,
    )


CHUNK = 128


def summed(out, put, *terms):
    def body(step, carry):
        rows = pl.ds(pl.multiple_of(step * CHUNK, CHUNK), CHUNK)
        total = terms[0](rows).astype(F32)
        for term in terms[1:]:
            total += term(rows).astype(F32)
        put(out, rows, total.astype(BF))
        return carry

    lax.fori_loop(0, out.shape[-2] // CHUNK, body, 0)


def plain(ref):
    return lambda rows: ref[rows, :]


def of(ref, n):
    return lambda rows: ref[n, rows, :]


def put_plain(out, rows, value):
    out[rows, :] = value


def put_at(n):
    def put(out, rows, value):
        out[n, rows, :] = value

    return put


def far_kernel_sum(far1, far3, low, high, out1, out3):
    half = low.shape[0]
    for ref, part, out, first in ((far1, low, out1, 0), (far3, high, out3, half)):
        for begin in range(0, 2 * half, CHUNK):
            rows = slice(begin, begin + CHUNK)
            if first <= begin < first + half:
                other = part[begin - first : begin - first + CHUNK].astype(F32)
                out[rows] = (ref[rows].astype(F32) + other).astype(BF)
            else:
                out[rows] = ref[rows]


def second_sum_kernel(far0, far1, far3, bf1, bf2, bf3, bh1, bh2, bh3, up, down, far):
    summed(up, put_at(0), plain(bf1), plain(bf2))
    summed(up, put_at(1), plain(bh1))
    summed(down, put_at(0), plain(bf3))
    summed(down, put_at(1), plain(bh3), plain(bh2))
    summed(far, put_plain, plain(far0), plain(far1), plain(far3))


def third_sum_kernel(bf0, bh0, up, down, before, behind):
    summed(before, put_plain, plain(bf0), of(up, 0), of(down, 0))
    summed(behind, put_plain, plain(bh0), of(up, 1), of(down, 1))


def scatter(grads, partials):
    far0, far1, far2_low, far2_high, far3 = grads(2, ())
    full = shape_of(far0.shape)
    pair = shape_of((2,) + far0.shape)
    far2_low, far2_high = send_y(far2_low, 1), send_y(far2_high, -1)
    bf0, bf1, bf2, bf3 = grads(1, (far0,))
    bh0, bh1, bh2, bh3 = grads(3, (bf0,))
    keep, send = partials((bh0,))

    far2_low, far2_high, bf2, bh2, send = after((far2_low, far2_high, bf2, bh2, send))
    bf2, bh2 = send_y(bf2, 1), send_y(bh2, -1)
    far1, far3 = call(far_kernel_sum, (far1, far3, far2_low, far2_high), [full] * 2)
    far1, far3 = send_y(far1, 1), send_y(far3, -1)
    core = send_mp(send, 0, 0, 1)
    part = shape_of((2,) + keep.shape[1:])
    near_x, far_x = call(core_sum_kernel, (keep, core), [part] * 2, moved=9 * MIB)
    far_x = send_x(far_x, 2)
    own0, own1, own2, own3 = grads(0, (core,))

    far1, far3, bf2, bh2 = after((far1, far3, bf2, bh2), own0)
    up, down, far = call(
        second_sum_kernel, (far0, far1, far3, bf1, bf2, bf3, bh1, bh2, bh3), [pair, pair, full]
    )
    up, down, far = send_y(up, 1), send_y(down, -1), send_z(far, 2)
    part = shape_of(keep.shape[1:])
    near_x, next_x = call(split_sum_kernel, (near_x, far_x), [part] * 2, moved=6 * MIB)
    next_x = send_x(next_x, 1)

    up, down, far, own1, own2, own3 = after((up, down, far, own1, own2, own3))
    before, behind = call(third_sum_kernel, (bf0, bh0, up, down), [full] * 2)
    own2 = send_y(own2, 2)
    own1, own3 = send_y(own1, 1), send_y(own3, -1)
    before, behind = send_z(before, 1), send_z(behind, -1)
    part = shape_of(keep.shape[2:])
    own, other = call(split_sum_kernel, (near_x, next_x), [part] * 2, moved=4 * MIB)
    return (own0, far, own1, own2, own3, before, behind), (own, send_mp(other, 1, 0, 0))


def local(
    dec_input,
    enc_output,
    query_weight,
    key_weight,
    value_weight,
    output_weight,
    cotangent,
    enc_lengths,
    dec_lengths,
):
    tokens, feat = dec_input.shape[1:]
    width = query_weight.shape[1]
    erows = enc_output.shape[1]
    keys = erows * NB
    scale = width ** (-0.5)
    unit = 2 * tokens * feat * width

    hbm = pl.BlockSpec(memory_space=pltpu.HBM)
    vmem = pl.BlockSpec(memory_space=pltpu.VMEM)
    weights, acts = pl.pallas_call(
        assemble_kernel,
        in_specs=[hbm] * 7,
        out_specs=[vmem] * 2,
        out_shape=[shape_of((feat, 4 * width)), shape_of((2 * tokens + keys, feat))],
        scratch_shapes=[
            pltpu.VMEM((width, feat), BF), pltpu.VMEM((erows, NB * feat), BF),
            pltpu.SemaphoreType.DMA((7,)),
        ],
        compiler_params=pltpu.CompilerParams(vmem_limit_bytes=56 * MIB),
    )(query_weight, key_weight, value_weight, output_weight, dec_input, cotangent, enc_output)
    own_group, near_group, far_group, pieces = gather(weights, acts)

    normed, masked, encoded, inv_rms = call(
        prepare_kernel, pieces,
        [
            shape_of((NB, tokens, feat)), shape_of((NB, tokens, feat)),
            shape_of((NB, keys, feat)), shape_of((tokens, 128), F32),
        ],
        (dec_lengths,), moved=12 * MIB,
    )
    stacked = (normed, masked, encoded)
    acc_shape = shape_of((4, tokens, width), F32)
    stack_shape = shape_of((4, feat, 4 * width))
    acc, own_stack = call(
        own_kernel, (*stacked, *own_group), [acc_shape, stack_shape],
        flops=16 * unit, moved=4 * MIB,
    )
    acc, near_stack = call(
        near_kernel, (*stacked, *near_group, acc),
        [acc_shape, shape_of((8, feat, 4 * width))], flops=32 * unit, moved=8 * MIB,
    )
    tshape, kshape = shape_of((tokens, width)), shape_of((keys, 2 * width))
    q_grad, kv_grad, attended, q_t, kv_t, at_t, stat, far_stack = call(
        functools.partial(far_kernel, scale), (*stacked, *far_group, acc),
        [
            tshape, kshape, tshape, shape_of((width, tokens)), shape_of((2 * width, keys)),
            shape_of((width, tokens)), shape_of((EXTRA, tokens)), stack_shape,
        ],
        (enc_lengths,), flops=24 * unit, moved=4 * MIB,
    )

    def grads(dz, others):
        (normed_in,) = after((normed,), *others) if others else (normed,)
        full, part = shape_of((4 * width, feat)), shape_of((2 * width, feat))
        outs = [full, full, part, part, full] if dz == 2 else [full] * 4
        return call(
            functools.partial(weight_grad_kernel, dz), (normed_in, masked, encoded, q_t, kv_t, at_t),
            outs, flops=16 * unit, moved=4 * MIB,
        )

    def partials(others):
        (q_in,) = after((q_grad,), *others)
        out = shape_of((4, 2, 3 * tokens + EXTRA, feat))
        return call(
            partial_kernel, (q_in, kv_grad, attended, stat, own_stack, near_stack, far_stack),
            [out, out], scratch=[pltpu.VMEM((keys, feat), BF)], flops=64 * unit, moved=14 * MIB,
        )

    shares, (line, got) = scatter(grads, partials)
    query_grad, key_grad, value_grad, output_grad = call_out(
        share_kernel, shares, [shape_of((feat, width))] * 4
    )
    stack = shape_of((1, tokens, feat))
    layer_out, input_grad, enc_grad = call_out(
        last_kernel, (line, got, acts, inv_rms),
        [stack, stack, shape_of((1, erows, NB * feat))], (dec_lengths,),
    )
    return (layer_out, input_grad, enc_grad, query_grad, key_grad, value_grad, output_grad)


def solution(mesh):
    in_specs = (
        P("dp", None, "mp"),
        P("dp", "mp", None),
        P("dp", "mp"),
        P("dp", "mp"),
        P("dp", "mp"),
        P("mp", "dp"),
        P("dp", None, "mp"),
        P("dp"),
        P("dp"),
    )
    out_specs = (
        P("dp", None, "mp"),
        P("dp", None, "mp"),
        P("dp", "mp", None),
        P("dp", "mp"),
        P("dp", "mp"),
        P("dp", "mp"),
        P("mp", "dp"),
    )
    return jax.shard_map(local, mesh=mesh, in_specs=in_specs, out_specs=out_specs, check_vma=False)
```

```python
import functools

import jax
import jax.numpy as jnp
from jax import lax
from jax.experimental import pallas as pl
from jax.experimental.pallas import tpu as pltpu
from jax.sharding import PartitionSpec as P

BF = jnp.bfloat16
F32 = jnp.float32
NB = 16
MIB = 1024 * 1024
COST = 16
EXTRA = 16

YZ = [(y, z) for y in range(4) for z in range(4)]
ZXC = [(a, b, c) for a in range(2) for b in range(4) for c in range(2)]


def dp_index(y, z):
    return (y % 4) * 4 + (z % 4)


def mp_index(a, b, c):
    return (a % 2) * 8 + (b % 4) * 2 + (c % 2)


def send_y(value, d):
    return lax.ppermute(value, "dp", [(dp_index(y, z), dp_index(y + d, z)) for y, z in YZ])


def send_z(value, d):
    return lax.ppermute(value, "dp", [(dp_index(y, z), dp_index(y, z + d)) for y, z in YZ])


def send_mp(value, da, db, dc):
    pairs = [(mp_index(a, b, c), mp_index(a + da, b + db, c + dc)) for a, b, c in ZXC]
    return lax.ppermute(value, "mp", pairs)


def send_x(value, bits):
    pairs = [(mp_index(a, b, c), mp_index(a, b ^ bits, c)) for a, b, c in ZXC]
    return lax.ppermute(value, "mp", pairs)


def nn(a, b):
    return lax.dot_general(a, b, (((1,), (0,)), ((), ())), preferred_element_type=F32)


def nt(a, b):
    return lax.dot_general(a, b, (((1,), (1,)), ((), ())), preferred_element_type=F32)


def tn(a, b):
    return lax.dot_general(a, b, (((0,), (0,)), ((), ())), preferred_element_type=F32)


def shape_of(shape, dtype=BF):
    return jax.ShapeDtypeStruct(shape, dtype)


def call(kernel, args, outs, scalars=(), scratch=(), flops=0, moved=0, vmem=8):
    spec = pl.BlockSpec(memory_space=pltpu.VMEM)
    return pl.pallas_call(
        kernel,
        in_specs=[pl.BlockSpec(memory_space=pltpu.SMEM)] * len(scalars) + [spec] * len(args),
        out_specs=[spec] * len(outs),
        out_shape=outs,
        scratch_shapes=scratch,
        compiler_params=pltpu.CompilerParams(vmem_limit_bytes=vmem * MIB),
        cost_estimate=pl.CostEstimate(flops=COST * flops, bytes_accessed=moved, transcendentals=0),
    )(*scalars, *args)


def call_out(kernel, args, outs, scalars=()):
    spec = pl.BlockSpec(memory_space=pltpu.VMEM)
    n = len(outs)

    def body(*refs):
        ins, results, sems = refs[: -2 * n - 1], refs[-2 * n - 1 : -n - 1], refs[-1]
        held = refs[-n - 1 : -1]
        kernel(*ins, *held)
        copies = [
            pltpu.make_async_copy(a, b, sems.at[k]) for k, (a, b) in enumerate(zip(held, results))
        ]
        for copy in copies:
            copy.start()
        for copy in copies:
            copy.wait()

    return pl.pallas_call(
        body,
        in_specs=[pl.BlockSpec(memory_space=pltpu.SMEM)] * len(scalars) + [spec] * len(args),
        out_specs=[pl.BlockSpec(memory_space=pltpu.HBM)] * n,
        out_shape=outs,
        scratch_shapes=[pltpu.VMEM(o.shape, o.dtype) for o in outs] + [pltpu.SemaphoreType.DMA((n,))],
        compiler_params=pltpu.CompilerParams(vmem_limit_bytes=8 * MIB),
    )(*scalars, *args)


def mp_place():
    place = lax.axis_index("mp")
    return lax.div(place, 8), lax.rem(lax.div(place, 2), 4), lax.rem(place, 2)


def dp_block(dy, dz):
    part = lax.axis_index("dp")
    return lax.rem(lax.div(part, 4) + dy, 4) * 4 + lax.rem(lax.rem(part, 4) + dz, 4)


def blocks_at(dz):
    return [dp_block(dy, dz) for dy in range(4)]


def after(values, *others):
    out = lax.optimization_barrier((others, tuple(values)))
    return out[1]


def pack_stat(row, shape):
    high = row.astype(BF).astype(F32)
    line = lax.broadcasted_iota(jnp.int32, shape, 0)
    rows = jnp.where(line == 0, high, jnp.where(line == 1, row - high, 0.0))
    return rows.astype(BF)


def stat_of(rows):
    return jnp.sum(rows.astype(F32), axis=0, keepdims=True)


def assemble_kernel(q_ref, k_ref, v_ref, o_ref, dec_ref, cot_ref, enc_ref, block_ref, acts_ref, o_buf, enc_buf, sems):
    width, feat = q_ref.shape[1], cot_ref.shape[2]
    tokens, erows = cot_ref.shape[1], enc_ref.shape[1]
    pairs = [(ref, block_ref.at[:, n * width : (n + 1) * width]) for n, ref in enumerate((q_ref, k_ref, v_ref))]
    pairs += [(o_ref, o_buf), (enc_ref.at[0], enc_buf)]
    pairs += [(dec_ref.at[0], acts_ref.at[:tokens]), (cot_ref.at[0], acts_ref.at[tokens : 2 * tokens])]
    copies = [pltpu.make_async_copy(a, b, sems.at[n]) for n, (a, b) in enumerate(pairs)]
    for copy in copies:
        copy.start()
    copies[3].wait()
    block_ref[:, 3 * width :] = o_buf[...].T
    copies[4].wait()
    for n in range(NB):
        line = 2 * tokens + n * erows
        acts_ref[line : line + erows] = enc_buf[:, n * feat : (n + 1) * feat]
    for n in (0, 1, 2, 5, 6):
        copies[n].wait()


def pair_kernel(first, second, out_ref):
    out_ref[0] = first[...]
    out_ref[1] = second[...]


def pick_kernel(first, second, out_first, out_second):
    out_first[...] = first[0]
    out_second[...] = second[1]


def join_kernel(first, second, out_ref):
    half = first.shape[0]
    out_ref[:half] = first[...]
    out_ref[half:] = second[...]


def halves_kernel(first, second, out_first, out_second):
    half = out_first.shape[0]
    out_first[...] = first[:half]
    out_second[...] = second[half:]


def quad_kernel(*refs):
    for n, ref in enumerate(refs[:4]):
        refs[4][n] = ref[...]


def prepare_kernel(len_ref, own_ref, other_ref, normed_ref, masked_ref, enc_ref, inv_ref):
    tokens, feat = normed_ref.shape[1:]
    erows = enc_ref.shape[1] // NB
    a, b, c = mp_place()
    square = jnp.zeros((tokens, 1), F32)
    for piece in (own_ref, other_ref):

        def add_squares(k, total, piece=piece):
            hidden = piece[lax.div(k, 2), lax.rem(k, 2), :tokens].astype(F32)
            return total + jnp.sum(hidden * hidden, axis=1, keepdims=True)

        square = lax.fori_loop(0, 8, add_squares, square)
    inv_rms = lax.rsqrt(square / (NB * feat) + 1e-06)
    inv_ref[...] = jnp.broadcast_to(inv_rms, inv_ref.shape)
    keep = lax.broadcasted_iota(jnp.int32, (tokens, feat), 0) < len_ref[0]
    for n, piece in enumerate((own_ref, other_ref)):

        def write(k, carry, n=n, piece=piece):
            x, z = lax.div(k, 2), lax.rem(k, 2)
            place = lax.rem(a + z, 2) * 8 + lax.rem(b + 4 - x, 4) * 2 + lax.rem(c + n, 2)
            normed_ref[place] = (piece[x, z, :tokens].astype(F32) * inv_ref[:, :1]).astype(BF)
            rows = piece[x, z, tokens : 2 * tokens]
            masked_ref[place] = jnp.where(keep, rows.astype(F32), 0.0).astype(BF)
            start = pl.multiple_of(place * erows, erows)
            for m in range(NB):
                line = 2 * tokens + m * erows
                enc_ref[m, pl.ds(start, erows), :] = piece[x, z, line : line + erows]
            return carry

        lax.fori_loop(0, 8, write, 0)


def attention(scale, enc_len, query, keyed, valued, attended_grad):
    scores = nt(query, keyed) * scale
    column = lax.broadcasted_iota(jnp.int32, scores.shape, 1)
    scores = jnp.where(column < enc_len, scores, -1e30)
    shifted = jnp.exp(scores - jnp.max(scores, axis=-1, keepdims=True))
    probs = shifted / jnp.sum(shifted, axis=-1, keepdims=True)
    probs_low = probs.astype(BF)
    attended = nn(probs_low, valued).astype(BF)
    probs_grad = nt(attended_grad, valued)
    inner = jnp.sum(probs * probs_grad, axis=-1, keepdims=True)
    scores_grad = (probs * (probs_grad - inner) * scale).astype(BF)
    q_grad = nn(scores_grad, keyed).astype(BF)
    k_grad = tn(scores_grad, query).astype(BF)
    v_grad = tn(probs_low, attended_grad).astype(BF)
    stat = jnp.sum(q_grad.astype(F32) * query.astype(F32), axis=-1, keepdims=True)
    return q_grad, k_grad, v_grad, attended, stat


def project(places, pieces, normed_ref, masked_ref, enc_ref, stack_ref, init):
    width = stack_ref.shape[2] // 4
    for n, piece in enumerate(pieces):
        stack_ref[n] = piece()
    out = init
    for n in range(0, len(pieces), 4):
        group = places[n : n + 4]
        rows = jnp.concatenate([stack_ref[n + k] for k in range(4)], axis=0)
        normed, enc, masked = (
            jnp.concatenate([ref[p] for p in group], axis=1)
            for ref in (normed_ref, enc_ref, masked_ref)
        )
        new = (
            nn(normed, rows[:, :width]),
            nn(enc, rows[:, width : 2 * width]),
            nn(enc, rows[:, 2 * width : 3 * width]),
            nn(masked, rows[:, 3 * width :]),
        )
        out = new if out is None else tuple(o + v for o, v in zip(out, new))
    return out


def one(ref):
    return lambda: ref[...]


def at(ref, n):
    return lambda: ref[n]


def both(low, high):
    return lambda: jnp.concatenate([low[...], high[...]], axis=0)


def own_kernel(normed_ref, masked_ref, enc_ref, *refs):
    own, high, low, across, acc_ref, stack_ref = refs
    pieces = [one(own), one(high), one(across), one(low)]
    acc = project(blocks_at(0), pieces, normed_ref, masked_ref, enc_ref, stack_ref, None)
    for n in range(4):
        acc_ref[n] = acc[n]


def near_kernel(normed_ref, masked_ref, enc_ref, *refs):
    pair, high, low, across_b, across_a, acc_in, acc_ref, stack_ref = refs
    pieces = [at(pair, 0), at(high, 0), one(across_b), at(low, 0)]
    pieces += [at(pair, 1), at(high, 1), one(across_a), at(low, 1)]
    places = blocks_at(3) + blocks_at(1)
    init = [acc_in[n] for n in range(4)]
    acc = project(places, pieces, normed_ref, masked_ref, enc_ref, stack_ref, init)
    for n in range(4):
        acc_ref[n] = acc[n]


def far_kernel(scale, len_ref, normed_ref, masked_ref, enc_ref, *refs):
    far, high, low, across_low, across_high, acc_in = refs[:6]
    kv_ref, qgt_ref, kvt_ref, att_ref, stat_ref, stack_ref = refs[6:]
    pieces = [one(far), one(high), both(across_low, across_high), one(low)]
    init = [acc_in[n] for n in range(4)]
    acc = project(blocks_at(2), pieces, normed_ref, masked_ref, enc_ref, stack_ref, init)
    out = attention(scale, len_ref[0], *(value.astype(BF) for value in acc))
    q_grad, k_grad, v_grad, attended, stat = out
    width = q_grad.shape[1]
    kv_ref[:, :width] = k_grad
    kv_ref[:, width:] = v_grad
    qgt_ref[...] = q_grad.T
    kvt_ref[:width] = k_grad.T
    kvt_ref[width:] = v_grad.T
    att_ref[...] = attended.T
    row = jnp.broadcast_to(stat, (stat.shape[0], 128)).T[0:1]
    stat_ref[...] = pack_stat(row, stat_ref.shape)


def weight_grad_kernel(dz, normed_ref, masked_ref, enc_ref, *refs):
    qgt_ref, kvt_ref, att_ref = refs[:3]
    outs = list(refs[3:])
    width = qgt_ref.shape[0]
    for n in range(4):
        place = dp_block(n, dz)
        query = nn(qgt_ref[...], normed_ref[place]).astype(BF)
        pair = nn(kvt_ref[...], enc_ref[place]).astype(BF)
        attn = nn(att_ref[...], masked_ref[place]).astype(BF)
        if n == 2 and len(outs) == 3:
            low, high = outs.pop(0), outs.pop(0)
            low[:width] = query
            low[width:] = pair[:width]
            high[:width] = pair[width:]
            high[width:] = attn
        else:
            out = outs.pop(0)
            out[:width] = query
            out[width : 3 * width] = pair
            out[3 * width :] = attn


def partial_kernel(side, q_t_ref, kv_ref, at_t_ref, stat_ref, own, near, far, out, kv_buf):
    width, tokens = q_t_ref.shape
    erows = kv_ref.shape[0] // NB
    a, b, c = mp_place()
    core = lax.rem(c + side, 2)
    for x in range(4):
        for z in range(2):
            out[z, x, 3 * tokens :, :] = stat_ref[...]
            owner = lax.rem(a + z, 2) * 8 + lax.bitwise_xor(b, x) * 2 + core
            start = pl.multiple_of(owner * erows, erows)
            line = (x * 2 + z) * erows
            kv_buf[line : line + erows, :] = kv_ref[pl.ds(start, erows), :]

    def block_of(n, shifts):
        return dp_block(lax.rem(n, 4), jnp.where(n < 4, shifts[0], shifts[1]))

    stacks = ((own, (0, 0)), (near, (3, 1)), (far, (2, 2)))
    for stack, shifts in stacks:

        def enc_part(n, carry, stack=stack, shifts=shifts):
            line = pl.multiple_of(2 * tokens + block_of(n, shifts) * erows, erows)
            enc = nt(kv_buf[...], stack[n, :, width : 3 * width]).astype(BF)
            for x in range(4):
                for z in range(2):
                    first = (x * 2 + z) * erows
                    out[z, x, pl.ds(line, erows), :] = enc[first : first + erows]
            return carry

        lax.fori_loop(0, stack.shape[0], enc_part, 0, unroll=2)

    odd = lax.rem(lax.axis_index("dp") + core, 2)
    for stack, shifts in stacks:

        @pl.when(odd == shifts[0] % 2)
        def _():
            def parts(n, carry):
                place = block_of(n, shifts)
                xr = lax.bitwise_xor(lax.rem(lax.div(place, 2), 4), b)
                zr = lax.rem(lax.div(place, 8) + 2 - a, 2)
                out[zr, xr, :tokens, :] = nn(stack[n, :, :width], q_t_ref[...]).astype(BF)
                out_part = nn(stack[n, :, 3 * width :], at_t_ref[...]).astype(BF)
                out[zr, xr, tokens : 2 * tokens, :] = out_part
                return carry

            lax.fori_loop(0, stack.shape[0], parts, 0, unroll=2)


def add_rows(ins, out):
    rows, feat = out.shape[0] - EXTRA, out.shape[1]

    def body(step, carry):
        part = pl.ds(pl.multiple_of(step * CHUNK, CHUNK), CHUNK)
        total = ins[0][part, :].astype(F32)
        for ref in ins[1:]:
            total += ref[part, :].astype(F32)
        out[part, :] = total.astype(BF)
        return carry

    lax.fori_loop(0, rows // CHUNK, body, 0)
    stat = stat_of(ins[0][rows:])
    for ref in ins[1:]:
        stat += stat_of(ref[rows:])
    out[rows:] = pack_stat(stat, (EXTRA, feat))


def core_sum_kernel(keep_ref, got_ref, *outs):
    for z, out in enumerate(outs):
        for x in range(4):
            add_rows([keep_ref.at[z, x], got_ref.at[z, x]], out.at[x])


def z_sum_kernel(keep_ref, got_ref, near_ref, far_ref):
    for x, out in enumerate((near_ref.at[0], near_ref.at[1], far_ref.at[0], far_ref.at[1])):
        add_rows([keep_ref.at[x], got_ref.at[x]], out)


def x_sum_kernel(first_ref, second_ref, *outs):
    for n, out in enumerate(outs):
        add_rows([first_ref.at[n], second_ref.at[n]], out)


def share_kernel(*refs):
    ins, outs = refs[:-4], refs[-4:]
    total = ins[0][...].astype(F32)
    for ref in ins[1:]:
        total += ref[...].astype(F32)
    total = total.astype(BF)
    width = outs[0].shape[1]
    for n, out in enumerate(outs[:3]):
        out[...] = total[n * width : (n + 1) * width].T
    outs[3][...] = total[3 * width :]


def last_kernel(len_ref, *refs):
    terms, (acts_ref, inv_ref, out_ref, in_ref, enc_ref) = refs[:2], refs[2:]
    tokens, feat = out_ref.shape[1:]
    rows = 3 * tokens
    total = [sum(ref[n * tokens : (n + 1) * tokens].astype(F32) for ref in terms) for n in range(3)]
    total[0], total[1] = total[0].T, total[1].T
    stat = sum(stat_of(ref[rows:]) for ref in terms)
    stat = jnp.broadcast_to(stat, (128, tokens)).T[:, :1] / (NB * feat)
    inv_rms = inv_ref[:, :1]
    dec = acts_ref[:tokens].astype(F32)
    out_ref[0] = (dec + total[1]).astype(BF)
    keep = lax.broadcasted_iota(jnp.int32, (tokens, feat), 0) < len_ref[0]
    masked = jnp.where(keep, acts_ref[tokens : 2 * tokens].astype(F32), 0.0)
    in_grad = masked + inv_rms * total[0] - dec * (inv_rms * inv_rms * stat)
    in_ref[0] = in_grad.astype(BF)
    erows = enc_ref.shape[1]
    for n in range(NB):
        enc_ref[0, :, n * feat : (n + 1) * feat] = total[2][n * erows : (n + 1) * erows].astype(BF)


def stack_pair(first, second):
    return call(pair_kernel, (first, second), [shape_of((2,) + first.shape)])[0]


def halves(first, second):
    half = shape_of((first.shape[0] // 2, first.shape[1]))
    return call(halves_kernel, (first, second), [half] * 2)


def gather(block, acts, begin):
    before, behind = send_z(block, 1), send_z(block, -1)
    low, high = send_y(block, 1), send_y(block, -1)
    other = send_mp(acts, 1, 0, 0)
    other, again = after((other, block), low, high)
    pair_acts = stack_pair(acts, other)
    x1, x3 = send_mp(pair_acts, 0, 1, 0), send_mp(pair_acts, 0, 3, 0)
    across = send_y(again, 2)

    pair_acts, x1, x3, before, behind = after((pair_acts, x1, x3, before, behind), across)
    x2 = send_mp(pair_acts, 0, 2, 0)
    pair = stack_pair(before, behind)
    pair_low, pair_high = send_y(pair, 1), send_y(pair, -1)
    to_low, to_high = halves(before, behind)
    far_low, far_high = send_z(to_low, 1), send_z(to_high, -1)
    (far,) = call(join_kernel, (far_low, far_high), [shape_of(block.shape)])
    f_low, f_high = send_y(far, 1), send_y(far, -1)

    x2, pair_low, pair_high, f_low, f_high = after((x2, pair_low, pair_high, f_low, f_high))
    (line,) = call(quad_kernel, (pair_acts, x1, x2, x3), [shape_of((4,) + pair_acts.shape)])
    sibling = send_mp(line, 0, 0, 1)
    to_low, to_high = call(pick_kernel, (pair_low, pair_high), [shape_of(block.shape)] * 2)
    across_b, across_a = send_y(to_low, 1), send_y(to_high, -1)
    to_low, to_high = halves(f_low, f_high)
    last_low, last_high = send_y(to_low, 1), send_y(to_high, -1)
    return (
        (pair, pair_high, pair_low, across_b, across_a),
        (far, f_high, f_low, last_low, last_high),
        begin((line, sibling), (block, high, low, across)),
    )


CHUNK = 128


def summed(out, put, *terms):
    def body(step, carry):
        rows = pl.ds(pl.multiple_of(step * CHUNK, CHUNK), CHUNK)
        total = terms[0](rows).astype(F32)
        for term in terms[1:]:
            total += term(rows).astype(F32)
        put(out, rows, total.astype(BF))
        return carry

    lax.fori_loop(0, out.shape[-2] // CHUNK, body, 0)


def plain(ref):
    return lambda rows: ref[rows, :]


def of(ref, n):
    return lambda rows: ref[n, rows, :]


def put_plain(out, rows, value):
    out[rows, :] = value


def put_at(n):
    def put(out, rows, value):
        out[n, rows, :] = value

    return put


def far_kernel_sum(far1, far3, low, high, out1, out3):
    half = low.shape[0]
    for ref, part, out, first in ((far1, low, out1, 0), (far3, high, out3, half)):
        for begin in range(0, 2 * half, CHUNK):
            rows = slice(begin, begin + CHUNK)
            if first <= begin < first + half:
                other = part[begin - first : begin - first + CHUNK].astype(F32)
                out[rows] = (ref[rows].astype(F32) + other).astype(BF)
            else:
                out[rows] = ref[rows]


def second_sum_kernel(far0, far1, far3, bf1, bf2, bf3, bh1, bh2, bh3, up, down, far_low, far_high):
    summed(up, put_at(0), plain(bf1), plain(bf2))
    summed(up, put_at(1), plain(bh1))
    summed(down, put_at(0), plain(bf3))
    summed(down, put_at(1), plain(bh3), plain(bh2))
    half = far_low.shape[0]
    for out, first in ((far_low, 0), (far_high, half)):
        summed(out, put_plain, *(plain(ref.at[first : first + half]) for ref in (far0, far1, far3)))


def third_sum_kernel(bf0, bh0, up, down, low, high, before, behind):
    half = low.shape[0]
    for out, ref, n, part, first in ((before, bf0, 0, low, 0), (behind, bh0, 1, high, half)):

        def body(step, carry, out=out, ref=ref, n=n, part=part, first=first):
            begin = pl.multiple_of(step * CHUNK, CHUNK)
            rows, here = pl.ds(begin + first, CHUNK), pl.ds(begin, CHUNK)
            rest = pl.ds(begin + half - first, CHUNK)
            total = ref[rows, :].astype(F32) + up[n, rows, :].astype(F32)
            total += down[n, rows, :].astype(F32) + part[here, :].astype(F32)
            out[rows, :] = total.astype(BF)
            total = ref[rest, :].astype(F32) + up[n, rest, :].astype(F32)
            total += down[n, rest, :].astype(F32)
            out[rest, :] = total.astype(BF)
            return carry

        lax.fori_loop(0, half // CHUNK, body, 0)


def scatter(grads, partials):
    send = partials(1)
    core = send_mp(send, 0, 0, 1)
    far0, far1, far2_low, far2_high, far3 = grads(2, (send,))
    full = shape_of(far0.shape)
    pair = shape_of((2,) + far0.shape)
    own0, own1, own2, own3 = grads(0, (far0,))
    far2_low, far2_high = send_y(far2_low, 1), send_y(far2_high, -1)
    bf0, bf1, bf2, bf3 = grads(1, (own0,))
    bh0, bh1, bh2, bh3 = grads(3, (bf0,))
    keep = partials(0)

    core, keep, far2_low, far2_high, bf2, bh2 = after(
        (core, keep, far2_low, far2_high, bf2, bh2)
    )
    part = shape_of(keep.shape[1:])
    own_z, other_z = call(core_sum_kernel, (keep, core), [part] * 2, moved=9 * MIB)
    other_z = send_mp(other_z, 1, 0, 0)
    bf2, bh2 = send_y(bf2, 1), send_y(bh2, -1)
    far1, far3 = call(far_kernel_sum, (far1, far3, far2_low, far2_high), [full] * 2)
    far1, far3 = send_y(far1, 1), send_y(far3, -1)

    far1, far3, bf2, bh2 = after((far1, far3, bf2, bh2))
    half = shape_of(far2_low.shape)
    up, down, far_low, far_high = call(
        second_sum_kernel, (far0, far1, far3, bf1, bf2, bf3, bh1, bh2, bh3),
        [pair, pair, half, half],
    )
    up, down = send_y(up, 1), send_y(down, -1)
    far_low, far_high = send_z(far_low, 1), send_z(far_high, -1)
    (other_z,) = after((other_z,), far_low, far_high)
    part = shape_of((2,) + keep.shape[2:])
    near_x, far_x = call(z_sum_kernel, (own_z, other_z), [part] * 2, moved=6 * MIB)
    far_x = send_x(far_x, 2)

    up, down, far_low, far_high, own1, own2, own3 = after(
        (up, down, far_low, far_high, own1, own2, own3)
    )
    before, behind = call(
        third_sum_kernel, (bf0, bh0, up, down, far_low, far_high), [full] * 2
    )
    before, behind = send_z(before, 1), send_z(behind, -1)
    own1, own3 = send_y(own1, 1), send_y(own3, -1)
    own2, own1, own3 = after((own2, own1, own3))
    own2 = send_y(own2, 2)
    part = shape_of(keep.shape[2:])
    own_x, next_x = call(x_sum_kernel, (near_x, far_x), [part] * 2, moved=3 * MIB)
    return (own0, own1, own2, own3, before, behind), (own_x, send_x(next_x, 1))


def local(
    dec_input,
    enc_output,
    query_weight,
    key_weight,
    value_weight,
    output_weight,
    cotangent,
    enc_lengths,
    dec_lengths,
):
    tokens, feat = dec_input.shape[1:]
    width = query_weight.shape[1]
    erows = enc_output.shape[1]
    keys = erows * NB
    scale = width ** (-0.5)
    unit = 2 * tokens * feat * width

    hbm = pl.BlockSpec(memory_space=pltpu.HBM)
    vmem = pl.BlockSpec(memory_space=pltpu.VMEM)
    weights, acts = pl.pallas_call(
        assemble_kernel,
        in_specs=[hbm] * 7,
        out_specs=[vmem] * 2,
        out_shape=[shape_of((feat, 4 * width)), shape_of((2 * tokens + keys, feat))],
        scratch_shapes=[
            pltpu.VMEM((width, feat), BF), pltpu.VMEM((erows, NB * feat), BF),
            pltpu.SemaphoreType.DMA((7,)),
        ],
        compiler_params=pltpu.CompilerParams(vmem_limit_bytes=56 * MIB),
    )(query_weight, key_weight, value_weight, output_weight, dec_input, cotangent, enc_output)
    acc_shape = shape_of((4, tokens, width), F32)
    stack_shape = shape_of((4, feat, 4 * width))

    def begin(pieces, own_group):
        normed, masked, encoded, inv_rms = call(
            prepare_kernel, pieces,
            [
                shape_of((NB, tokens, feat)), shape_of((NB, tokens, feat)),
                shape_of((NB, keys, feat)), shape_of((tokens, 128), F32),
            ],
            (dec_lengths,), moved=12 * MIB,
        )
        acc, own_stack = call(
            own_kernel, (normed, masked, encoded, *own_group), [acc_shape, stack_shape],
            flops=16 * unit, moved=4 * MIB,
        )
        return normed, masked, encoded, inv_rms, own_stack, acc

    near_group, far_group, start = gather(weights, acts, begin)
    normed, masked, encoded, inv_rms, own_stack, acc = start
    stacked = (normed, masked, encoded)
    acc, near_stack = call(
        near_kernel, (*stacked, *near_group, acc), [acc_shape, shape_of((8, feat, 4 * width))],
        flops=32 * unit, moved=8 * MIB,
    )
    kshape = shape_of((keys, 2 * width))
    kv_grad, q_t, kv_t, at_t, stat, far_stack = call(
        functools.partial(far_kernel, scale), (*stacked, *far_group, acc),
        [
            kshape, shape_of((width, tokens)), shape_of((2 * width, keys)),
            shape_of((width, tokens)), shape_of((EXTRA, tokens)), stack_shape,
        ],
        (enc_lengths,), flops=24 * unit, moved=4 * MIB,
    )

    def grads(dz, others):
        (normed_in,) = after((normed,), *others) if others else (normed,)
        full, part = shape_of((4 * width, feat)), shape_of((2 * width, feat))
        outs = [full, full, part, part, full] if dz == 2 else [full] * 4
        return call(
            functools.partial(weight_grad_kernel, dz), (normed_in, masked, encoded, q_t, kv_t, at_t),
            outs, flops=16 * unit, moved=4 * MIB,
        )

    def partials(side):
        out = shape_of((2, 4, 3 * tokens + EXTRA, feat))
        return call(
            functools.partial(partial_kernel, side),
            (q_t, kv_grad, at_t, stat, own_stack, near_stack, far_stack),
            [out], scratch=[pltpu.VMEM((keys // 2, 2 * width), BF)], flops=32 * unit, moved=14 * MIB,
        )[0]

    shares, terms = scatter(grads, partials)
    query_grad, key_grad, value_grad, output_grad = call_out(
        share_kernel, shares, [shape_of((feat, width))] * 4
    )
    stack = shape_of((1, tokens, feat))
    layer_out, input_grad, enc_grad = call_out(
        last_kernel, (*terms, acts, inv_rms),
        [stack, stack, shape_of((1, erows, NB * feat))], (dec_lengths,),
    )
    return (layer_out, input_grad, enc_grad, query_grad, key_grad, value_grad, output_grad)


def solution(mesh):
    in_specs = (
        P("dp", None, "mp"),
        P("dp", "mp", None),
        P("dp", "mp"),
        P("dp", "mp"),
        P("dp", "mp"),
        P("mp", "dp"),
        P("dp", None, "mp"),
        P("dp"),
        P("dp"),
    )
    out_specs = (
        P("dp", None, "mp"),
        P("dp", None, "mp"),
        P("dp", "mp", None),
        P("dp", "mp"),
        P("dp", "mp"),
        P("dp", "mp"),
        P("mp", "dp"),
    )
    return jax.shard_map(local, mesh=mesh, in_specs=in_specs, out_specs=out_specs, check_vma=False)
```

```python
import functools

import jax
import jax.numpy as jnp
from jax import lax
from jax.experimental import pallas as pl
from jax.experimental.pallas import tpu as pltpu
from jax.sharding import PartitionSpec as P

BF = jnp.bfloat16
F32 = jnp.float32
NB = 16
MIB = 1024 * 1024
COST = 16
EXTRA = 16

YZ = [(y, z) for y in range(4) for z in range(4)]
ZXC = [(a, b, c) for a in range(2) for b in range(4) for c in range(2)]


def dp_index(y, z):
    return (y % 4) * 4 + (z % 4)


def mp_index(a, b, c):
    return (a % 2) * 8 + (b % 4) * 2 + (c % 2)


def send_y(value, d):
    return lax.ppermute(value, "dp", [(dp_index(y, z), dp_index(y + d, z)) for y, z in YZ])


def send_z(value, d):
    return lax.ppermute(value, "dp", [(dp_index(y, z), dp_index(y, z + d)) for y, z in YZ])


def send_mp(value, da, db, dc):
    pairs = [(mp_index(a, b, c), mp_index(a + da, b + db, c + dc)) for a, b, c in ZXC]
    return lax.ppermute(value, "mp", pairs)


def send_x(value, bits):
    pairs = [(mp_index(a, b, c), mp_index(a, b ^ bits, c)) for a, b, c in ZXC]
    return lax.ppermute(value, "mp", pairs)


def nn(a, b):
    return lax.dot_general(a, b, (((1,), (0,)), ((), ())), preferred_element_type=F32)


def nt(a, b):
    return lax.dot_general(a, b, (((1,), (1,)), ((), ())), preferred_element_type=F32)


def tn(a, b):
    return lax.dot_general(a, b, (((0,), (0,)), ((), ())), preferred_element_type=F32)


def shape_of(shape, dtype=BF):
    return jax.ShapeDtypeStruct(shape, dtype)


def call(kernel, args, outs, scalars=(), scratch=(), flops=0, moved=0, vmem=8, aliases=()):
    spec = pl.BlockSpec(memory_space=pltpu.VMEM)
    return pl.pallas_call(
        kernel,
        in_specs=[pl.BlockSpec(memory_space=pltpu.SMEM)] * len(scalars) + [spec] * len(args),
        out_specs=[spec] * len(outs),
        out_shape=outs,
        scratch_shapes=scratch,
        input_output_aliases=dict(aliases),
        compiler_params=pltpu.CompilerParams(vmem_limit_bytes=vmem * MIB),
        cost_estimate=pl.CostEstimate(flops=COST * flops, bytes_accessed=moved, transcendentals=0),
    )(*scalars, *args)


def call_out(kernel, args, outs, scalars=()):
    spec = pl.BlockSpec(memory_space=pltpu.VMEM)
    n = len(outs)

    def body(*refs):
        ins, results, sems = refs[: -2 * n - 1], refs[-2 * n - 1 : -n - 1], refs[-1]
        held = refs[-n - 1 : -1]
        kernel(*ins, *held)
        copies = [
            pltpu.make_async_copy(a, b, sems.at[k]) for k, (a, b) in enumerate(zip(held, results))
        ]
        for copy in copies:
            copy.start()
        for copy in copies:
            copy.wait()

    return pl.pallas_call(
        body,
        in_specs=[pl.BlockSpec(memory_space=pltpu.SMEM)] * len(scalars) + [spec] * len(args),
        out_specs=[pl.BlockSpec(memory_space=pltpu.HBM)] * n,
        out_shape=outs,
        scratch_shapes=[pltpu.VMEM(o.shape, o.dtype) for o in outs] + [pltpu.SemaphoreType.DMA((n,))],
        compiler_params=pltpu.CompilerParams(vmem_limit_bytes=8 * MIB),
    )(*scalars, *args)


def mp_place():
    place = lax.axis_index("mp")
    return lax.div(place, 8), lax.rem(lax.div(place, 2), 4), lax.rem(place, 2)


def dp_block(dy, dz):
    part = lax.axis_index("dp")
    return lax.rem(lax.div(part, 4) + dy, 4) * 4 + lax.rem(lax.rem(part, 4) + dz, 4)


def blocks_at(dz):
    return [dp_block(dy, dz) for dy in range(4)]


def after(values, *others):
    out = lax.optimization_barrier((others, tuple(values)))
    return out[1]


def pack_stat(row, shape):
    high = row.astype(BF).astype(F32)
    line = lax.broadcasted_iota(jnp.int32, shape, 0)
    rows = jnp.where(line == 0, high, jnp.where(line == 1, row - high, 0.0))
    return rows.astype(BF)


def stat_of(rows):
    return jnp.sum(rows.astype(F32), axis=0, keepdims=True)


def assemble_kernel(q_ref, k_ref, v_ref, o_ref, dec_ref, cot_ref, enc_ref, block_ref, acts_ref, o_buf, enc_buf, sems):
    width, feat = q_ref.shape[1], cot_ref.shape[2]
    tokens, erows = cot_ref.shape[1], enc_ref.shape[1]
    pairs = [(ref, block_ref.at[:, n * width : (n + 1) * width]) for n, ref in enumerate((q_ref, k_ref, v_ref))]
    pairs += [(o_ref, o_buf), (enc_ref.at[0], enc_buf)]
    pairs += [(dec_ref.at[0], acts_ref.at[:tokens]), (cot_ref.at[0], acts_ref.at[tokens : 2 * tokens])]
    copies = [pltpu.make_async_copy(a, b, sems.at[n]) for n, (a, b) in enumerate(pairs)]
    for copy in copies:
        copy.start()
    copies[3].wait()
    block_ref[:, 3 * width :] = o_buf[...].T
    copies[4].wait()
    for n in range(NB):
        line = 2 * tokens + n * erows
        acts_ref[line : line + erows] = enc_buf[:, n * feat : (n + 1) * feat]
    for n in (0, 1, 2, 5, 6):
        copies[n].wait()


def pair_kernel(first, second, out_ref):
    out_ref[0] = first[...]
    out_ref[1] = second[...]


def pick_kernel(first, second, out_first, out_second):
    out_first[...] = first[0]
    out_second[...] = second[1]


def join_kernel(first, second, out_ref):
    half = first.shape[0]
    out_ref[:half] = first[...]
    out_ref[half:] = second[...]


def halves_kernel(first, second, out_first, out_second):
    half = out_first.shape[0]
    out_first[...] = first[:half]
    out_second[...] = second[half:]


def quad_kernel(*refs):
    for n, ref in enumerate(refs[:4]):
        refs[4][n] = ref[...]


def prepare_kernel(len_ref, own_ref, other_ref, normed_ref, masked_ref, enc_ref, inv_ref):
    tokens, feat = normed_ref.shape[1:]
    erows = enc_ref.shape[1] // NB
    a, b, c = mp_place()
    square = jnp.zeros((tokens, 1), F32)
    for piece in (own_ref, other_ref):

        def add_squares(k, total, piece=piece):
            hidden = piece[lax.div(k, 4), lax.rem(k, 4), :tokens].astype(F32)
            return total + jnp.sum(hidden * hidden, axis=1, keepdims=True)

        square = lax.fori_loop(0, 8, add_squares, square)
    inv_rms = lax.rsqrt(square / (NB * feat) + 1e-06)
    inv_ref[...] = jnp.broadcast_to(inv_rms, inv_ref.shape)
    keep = lax.broadcasted_iota(jnp.int32, (tokens, feat), 0) < len_ref[0]
    for n, piece in enumerate((own_ref, other_ref)):

        def write(k, carry, n=n, piece=piece):
            z, x = lax.div(k, 4), lax.rem(k, 4)
            place = lax.rem(a + z, 2) * 8 + lax.rem(b + 4 - x, 4) * 2 + lax.rem(c + n, 2)
            normed_ref[place] = (piece[z, x, :tokens].astype(F32) * inv_ref[:, :1]).astype(BF)
            rows = piece[z, x, tokens : 2 * tokens]
            masked_ref[place] = jnp.where(keep, rows.astype(F32), 0.0).astype(BF)
            start = pl.multiple_of(place * erows, erows)
            for m in range(NB):
                line = 2 * tokens + m * erows
                enc_ref[m, pl.ds(start, erows), :] = piece[z, x, line : line + erows]
            return carry

        lax.fori_loop(0, 8, write, 0)


def attention(scale, enc_len, query, keyed, valued, attended_grad):
    scores = nt(query, keyed) * scale
    column = lax.broadcasted_iota(jnp.int32, scores.shape, 1)
    scores = jnp.where(column < enc_len, scores, -1e30)
    shifted = jnp.exp(scores - jnp.max(scores, axis=-1, keepdims=True))
    probs = shifted / jnp.sum(shifted, axis=-1, keepdims=True)
    probs_low = probs.astype(BF)
    attended = nn(probs_low, valued).astype(BF)
    probs_grad = nt(attended_grad, valued)
    inner = jnp.sum(probs * probs_grad, axis=-1, keepdims=True)
    scores_grad = (probs * (probs_grad - inner) * scale).astype(BF)
    q_grad = nn(scores_grad, keyed).astype(BF)
    k_grad = tn(scores_grad, query).astype(BF)
    v_grad = tn(probs_low, attended_grad).astype(BF)
    stat = jnp.sum(q_grad.astype(F32) * query.astype(F32), axis=-1, keepdims=True)
    return q_grad, k_grad, v_grad, attended, stat


def project(places, pieces, normed_ref, masked_ref, enc_ref, stack_ref, init, first=0):
    width = stack_ref.shape[2] // 4
    for n, piece in enumerate(pieces):
        stack_ref[first + n] = piece()
    out = init
    for n in range(0, len(pieces), 4):
        group = places[n : n + 4]
        rows = jnp.concatenate([stack_ref[first + n + k] for k in range(4)], axis=0)
        normed, enc, masked = (
            jnp.concatenate([ref[p] for p in group], axis=1)
            for ref in (normed_ref, enc_ref, masked_ref)
        )
        new = (
            nn(normed, rows[:, :width]),
            nn(enc, rows[:, width : 2 * width]),
            nn(enc, rows[:, 2 * width : 3 * width]),
            nn(masked, rows[:, 3 * width :]),
        )
        out = new if out is None else tuple(o + v for o, v in zip(out, new))
    return out


def one(ref):
    return lambda: ref[...]


def at(ref, n):
    return lambda: ref[n]


def both(low, high):
    return lambda: jnp.concatenate([low[...], high[...]], axis=0)


def own_kernel(normed_ref, masked_ref, enc_ref, *refs):
    own, high, low, across, acc_ref, stack_ref = refs
    pieces = [one(own), one(high), one(across), one(low)]
    acc = project(blocks_at(0), pieces, normed_ref, masked_ref, enc_ref, stack_ref, None)
    for n in range(4):
        acc_ref[n] = acc[n]


def near_kernel(normed_ref, masked_ref, enc_ref, *refs):
    pair, high, low, across_b, across_a, acc_in, acc_ref, stack_ref = refs
    pieces = [at(pair, 0), at(high, 0), one(across_b), at(low, 0)]
    pieces += [at(pair, 1), at(high, 1), one(across_a), at(low, 1)]
    width = stack_ref.shape[2] // 4
    for n, piece in enumerate(pieces):
        stack_ref[n] = piece()
    for n in range(4):
        acc_ref[n] = acc_in[n]

    def body(group, carry):
        places = [dp_block(dy, 3 - 2 * group) for dy in range(4)]
        rows = jnp.concatenate([stack_ref[4 * group + k] for k in range(4)], axis=0)
        normed, enc, masked = (
            jnp.concatenate([ref[p] for p in places], axis=1)
            for ref in (normed_ref, enc_ref, masked_ref)
        )
        for n, left in enumerate((normed, enc, enc, masked)):
            acc_ref[n] += nn(left, rows[:, n * width : (n + 1) * width])
        return carry

    lax.fori_loop(0, 2, body, 0)


def far_kernel(scale, len_ref, normed_ref, masked_ref, enc_ref, *refs):
    far, high, low, across_low, across_high, acc_in = refs[:6]
    kv_ref, qgt_ref, kvt_ref, att_ref, stat_ref, stack_ref = refs[7:]
    pieces = [one(far), one(high), both(across_low, across_high), one(low)]
    init = [acc_in[n] for n in range(4)]
    acc = project(blocks_at(2), pieces, normed_ref, masked_ref, enc_ref, stack_ref, init, 4)
    out = attention(scale, len_ref[0], *(value.astype(BF) for value in acc))
    q_grad, k_grad, v_grad, attended, stat = out
    width = q_grad.shape[1]
    kv_ref[:, :width] = k_grad
    kv_ref[:, width:] = v_grad
    qgt_ref[...] = q_grad.T
    kvt_ref[:width] = k_grad.T
    kvt_ref[width:] = v_grad.T
    att_ref[...] = attended.T
    row = jnp.broadcast_to(stat, (stat.shape[0], 128)).T[0:1]
    stat_ref[...] = pack_stat(row, stat_ref.shape)


def weight_grad_kernel(dz, normed_ref, masked_ref, enc_ref, *refs):
    qgt_ref, kvt_ref, att_ref = refs[:3]
    outs, held = refs[3:-1], refs[-1]
    width = qgt_ref.shape[0]
    targets = [outs[0], outs[1], outs[2:-1], outs[-1]]

    def body(n, carry):
        place = dp_block(n, dz)
        held[:width] = nn(qgt_ref[...], normed_ref[place]).astype(BF)
        held[width : 3 * width] = nn(kvt_ref[...], enc_ref[place]).astype(BF)
        held[3 * width :] = nn(att_ref[...], masked_ref[place]).astype(BF)
        for k, target in enumerate(targets):

            @pl.when(n == k)
            def _():
                parts = target if isinstance(target, tuple) else (target,)
                first = 0
                for part in parts:
                    part[...] = held[first : first + part.shape[0]]
                    first += part.shape[0]

        return carry

    lax.fori_loop(0, 4, body, 0)


def partial_kernel(side, q_t_ref, kv_ref, at_t_ref, stat_ref, even, odd, out, kv_buf):
    width, tokens = q_t_ref.shape
    erows = kv_ref.shape[0] // NB
    a, b, c = mp_place()
    core = lax.rem(c + side, 2)
    for x in range(4):
        for z in range(2):
            out[z, x, 3 * tokens :, :] = stat_ref[...]
            owner = lax.rem(a + z, 2) * 8 + lax.bitwise_xor(b, x) * 2 + core
            start = pl.multiple_of(owner * erows, erows)
            line = (x * 2 + z) * erows
            kv_buf[line : line + erows, :] = kv_ref[pl.ds(start, erows), :]

    def block_of(n, shifts):
        return dp_block(lax.rem(n, 4), jnp.where(n < 4, shifts[0], shifts[1]))

    stacks = ((even, (0, 2)), (odd, (3, 1)))
    for stack, shifts in stacks:

        def enc_part(n, carry, stack=stack, shifts=shifts):
            line = pl.multiple_of(2 * tokens + block_of(n, shifts) * erows, erows)
            enc = nt(kv_buf[...], stack[n, :, width : 3 * width]).astype(BF)
            for x in range(4):
                for z in range(2):
                    first = (x * 2 + z) * erows
                    out[z, x, pl.ds(line, erows), :] = enc[first : first + erows]
            return carry

        lax.fori_loop(0, stack.shape[0], enc_part, 0, unroll=2)

    last = lax.rem(lax.axis_index("dp") + core, 2)
    for stack, shifts in stacks:

        @pl.when(last == shifts[0] % 2)
        def _():
            def parts(n, carry):
                place = block_of(n, shifts)
                xr = lax.bitwise_xor(lax.rem(lax.div(place, 2), 4), b)
                zr = lax.rem(lax.div(place, 8) + 2 - a, 2)
                out[zr, xr, :tokens, :] = nn(stack[n, :, :width], q_t_ref[...]).astype(BF)
                out_part = nn(stack[n, :, 3 * width :], at_t_ref[...]).astype(BF)
                out[zr, xr, tokens : 2 * tokens, :] = out_part
                return carry

            lax.fori_loop(0, stack.shape[0], parts, 0, unroll=2)


def add_rows(ins, out):
    rows, feat = out.shape[0] - EXTRA, out.shape[1]

    def body(step, carry):
        part = pl.ds(pl.multiple_of(step * CHUNK, CHUNK), CHUNK)
        total = ins[0][part, :].astype(F32)
        for ref in ins[1:]:
            total += ref[part, :].astype(F32)
        out[part, :] = total.astype(BF)
        return carry

    lax.fori_loop(0, rows // CHUNK, body, 0)
    stat = stat_of(ins[0][rows:])
    for ref in ins[1:]:
        stat += stat_of(ref[rows:])
    out[rows:] = pack_stat(stat, (EXTRA, feat))


def core_sum_kernel(keep_ref, got_ref, *outs):
    for z, out in enumerate(outs):

        def body(x, carry, z=z, out=out):
            add_rows([keep_ref.at[z, x], got_ref.at[z, x]], out.at[x])
            return carry

        lax.fori_loop(0, 4, body, 0)


def z_sum_kernel(keep_ref, got_ref, *outs):
    for n, out in enumerate(outs):

        def body(x, carry, n=n, out=out):
            add_rows([keep_ref.at[2 * n + x], got_ref.at[2 * n + x]], out.at[x])
            return carry

        lax.fori_loop(0, 2, body, 0)


def x_sum_kernel(first_ref, second_ref, *outs):
    for n, out in enumerate(outs):
        add_rows([first_ref.at[n], second_ref.at[n]], out)


def share_kernel(*refs):
    ins, outs = refs[:-4], refs[-4:]
    total = ins[0][...].astype(F32)
    for ref in ins[1:]:
        total += ref[...].astype(F32)
    total = total.astype(BF)
    width = outs[0].shape[1]
    for n, out in enumerate(outs[:3]):
        out[...] = total[n * width : (n + 1) * width].T
    outs[3][...] = total[3 * width :]


def last_kernel(len_ref, *refs):
    terms, (acts_ref, inv_ref, out_ref, in_ref, enc_ref) = refs[:2], refs[2:]
    tokens, feat = out_ref.shape[1:]
    rows = 3 * tokens
    total = [sum(ref[n * tokens : (n + 1) * tokens].astype(F32) for ref in terms) for n in range(3)]
    total[0], total[1] = total[0].T, total[1].T
    stat = sum(stat_of(ref[rows:]) for ref in terms)
    stat = jnp.broadcast_to(stat, (128, tokens)).T[:, :1] / (NB * feat)
    inv_rms = inv_ref[:, :1]
    dec = acts_ref[:tokens].astype(F32)
    out_ref[0] = (dec + total[1]).astype(BF)
    keep = lax.broadcasted_iota(jnp.int32, (tokens, feat), 0) < len_ref[0]
    masked = jnp.where(keep, acts_ref[tokens : 2 * tokens].astype(F32), 0.0)
    in_grad = masked + inv_rms * total[0] - dec * (inv_rms * inv_rms * stat)
    in_ref[0] = in_grad.astype(BF)
    erows = enc_ref.shape[1]
    for n in range(NB):
        enc_ref[0, :, n * feat : (n + 1) * feat] = total[2][n * erows : (n + 1) * erows].astype(BF)


def stack_pair(first, second):
    return call(pair_kernel, (first, second), [shape_of((2,) + first.shape)])[0]


def halves(first, second):
    half = shape_of((first.shape[0] // 2, first.shape[1]))
    return call(halves_kernel, (first, second), [half] * 2)


def gather(block, acts, begin):
    x1, x3 = send_mp(acts, 0, 1, 0), send_mp(acts, 0, 3, 0)
    before, behind = send_z(block, 1), send_z(block, -1)
    low, high = send_y(block, 1), send_y(block, -1)
    x1, x3, to_x2, again = after((x1, x3, acts, block), low, high)
    x2 = send_mp(to_x2, 0, 2, 0)
    across = send_y(again, 2)

    x1, x2, x3, before, behind = after((x1, x2, x3, before, behind), across)
    (quad,) = call(quad_kernel, (acts, x1, x2, x3), [shape_of((4,) + acts.shape)])
    pair = stack_pair(before, behind)
    pair_low, pair_high = send_y(pair, 1), send_y(pair, -1)
    to_low, to_high = halves(before, behind)
    far_low, far_high = send_z(to_low, 1), send_z(to_high, -1)
    (to_other,) = after((quad,), far_low, far_high)
    other = send_mp(to_other, 1, 0, 0)

    pair_low, pair_high, far_low, far_high = after((pair_low, pair_high, far_low, far_high))
    (far,) = call(join_kernel, (far_low, far_high), [shape_of(block.shape)])
    f_low, f_high = send_y(far, 1), send_y(far, -1)
    to_low, to_high = call(pick_kernel, (pair_low, pair_high), [shape_of(block.shape)] * 2)
    across_b, across_a = send_y(to_low, 1), send_y(to_high, -1)

    quad, other, f_low, f_high = after((quad, other, f_low, f_high), across_a, across_b)
    (line,) = call(pair_kernel, (quad, other), [shape_of((2,) + quad.shape)])
    sibling = send_mp(line, 0, 0, 1)
    to_low, to_high = halves(f_low, f_high)
    last_low, last_high = send_y(to_low, 1), send_y(to_high, -1)
    return (
        (pair, pair_high, pair_low, across_b, across_a),
        (far, f_high, f_low, last_low, last_high),
        begin((line, sibling), (block, high, low, across)),
    )


CHUNK = 128


def summed(out, put, *terms):
    def body(step, carry):
        rows = pl.ds(pl.multiple_of(step * CHUNK, CHUNK), CHUNK)
        total = terms[0](rows).astype(F32)
        for term in terms[1:]:
            total += term(rows).astype(F32)
        put(out, rows, total.astype(BF))
        return carry

    lax.fori_loop(0, out.shape[-2] // CHUNK, body, 0)


def plain(ref):
    return lambda rows: ref[rows, :]


def of(ref, n):
    return lambda rows: ref[n, rows, :]


def put_plain(out, rows, value):
    out[rows, :] = value


def put_at(n):
    def put(out, rows, value):
        out[n, rows, :] = value

    return put


def far_kernel_sum(far1, far3, low, high, out1, out3):
    half = low.shape[0]
    for ref, part, out, first in ((far1, low, out1, 0), (far3, high, out3, half)):
        rest = slice(half - first, 2 * half - first)
        out[rest] = ref[rest]
        here = ref.at[first : first + half]
        summed(out.at[first : first + half], put_plain, plain(here), plain(part))


def second_sum_kernel(far0, far1, far3, bf1, bf2, bf3, bh1, bh2, bh3, up, down, far_low, far_high):
    summed(up, put_at(0), plain(bf1), plain(bf2))
    summed(up, put_at(1), plain(bh1))
    summed(down, put_at(0), plain(bf3))
    summed(down, put_at(1), plain(bh3), plain(bh2))
    half = far_low.shape[0]
    for out, first in ((far_low, 0), (far_high, half)):
        summed(out, put_plain, *(plain(ref.at[first : first + half]) for ref in (far0, far1, far3)))


def third_sum_kernel(bf0, bh0, up, down, low, high, before, behind):
    half = low.shape[0]
    for out, ref, n, part, first in ((before, bf0, 0, low, 0), (behind, bh0, 1, high, half)):

        def body(step, carry, out=out, ref=ref, n=n, part=part, first=first):
            begin = pl.multiple_of(step * CHUNK, CHUNK)
            rows, here = pl.ds(begin + first, CHUNK), pl.ds(begin, CHUNK)
            rest = pl.ds(begin + half - first, CHUNK)
            total = ref[rows, :].astype(F32) + up[n, rows, :].astype(F32)
            total += down[n, rows, :].astype(F32) + part[here, :].astype(F32)
            out[rows, :] = total.astype(BF)
            total = ref[rest, :].astype(F32) + up[n, rest, :].astype(F32)
            total += down[n, rest, :].astype(F32)
            out[rest, :] = total.astype(BF)
            return carry

        lax.fori_loop(0, half // CHUNK, body, 0)


def scatter(grads, partials):
    send = partials(1)
    core = send_mp(send, 0, 0, 1)
    far0, far1, far2_low, far2_high, far3 = grads(2, (send,))
    full = shape_of(far0.shape)
    pair = shape_of((2,) + far0.shape)
    own0, own1, own2, own3 = grads(0, (far0,))
    far2_low, far2_high = send_y(far2_low, 1), send_y(far2_high, -1)
    bf0, bf1, bf2, bf3 = grads(1, (own0,))
    bh0, bh1, bh2, bh3 = grads(3, (bf0,))
    keep = partials(0)

    core, keep, far2_low, far2_high, bf2, bh2 = after(
        (core, keep, far2_low, far2_high, bf2, bh2)
    )
    part = shape_of(keep.shape[1:])
    own_z, other_z = call(core_sum_kernel, (keep, core), [part] * 2, moved=9 * MIB)
    other_z = send_mp(other_z, 1, 0, 0)
    bf2, bh2 = send_y(bf2, 1), send_y(bh2, -1)
    far1, far3 = call(far_kernel_sum, (far1, far3, far2_low, far2_high), [full] * 2)
    far1, far3 = send_y(far1, 1), send_y(far3, -1)

    far1, far3, bf2, bh2 = after((far1, far3, bf2, bh2))
    half = shape_of(far2_low.shape)
    up, down, far_low, far_high = call(
        second_sum_kernel, (far0, far1, far3, bf1, bf2, bf3, bh1, bh2, bh3),
        [pair, pair, half, half],
    )
    up, down = send_y(up, 1), send_y(down, -1)
    far_low, far_high = send_z(far_low, 1), send_z(far_high, -1)
    (other_z,) = after((other_z,), far_low, far_high)
    part = shape_of((2,) + keep.shape[2:])
    near_x, far_x = call(z_sum_kernel, (own_z, other_z), [part] * 2, moved=6 * MIB)
    far_x = send_x(far_x, 2)

    up, down, far_low, far_high, own1, own2, own3 = after(
        (up, down, far_low, far_high, own1, own2, own3)
    )
    before, behind = call(
        third_sum_kernel, (bf0, bh0, up, down, far_low, far_high), [full] * 2
    )
    before, behind = send_z(before, 1), send_z(behind, -1)
    own1, own3 = send_y(own1, 1), send_y(own3, -1)
    own2, own1, own3 = after((own2, own1, own3))
    own2 = send_y(own2, 2)
    part = shape_of(keep.shape[2:])
    own_x, next_x = call(x_sum_kernel, (near_x, far_x), [part] * 2, moved=3 * MIB)
    return (own0, own1, own2, own3, before, behind), (own_x, send_x(next_x, 1))


def local(
    dec_input,
    enc_output,
    query_weight,
    key_weight,
    value_weight,
    output_weight,
    cotangent,
    enc_lengths,
    dec_lengths,
):
    tokens, feat = dec_input.shape[1:]
    width = query_weight.shape[1]
    erows = enc_output.shape[1]
    keys = erows * NB
    scale = width ** (-0.5)
    unit = 2 * tokens * feat * width

    hbm = pl.BlockSpec(memory_space=pltpu.HBM)
    vmem = pl.BlockSpec(memory_space=pltpu.VMEM)
    weights, acts = pl.pallas_call(
        assemble_kernel,
        in_specs=[hbm] * 7,
        out_specs=[vmem] * 2,
        out_shape=[shape_of((feat, 4 * width)), shape_of((2 * tokens + keys, feat))],
        scratch_shapes=[
            pltpu.VMEM((width, feat), BF), pltpu.VMEM((erows, NB * feat), BF),
            pltpu.SemaphoreType.DMA((7,)),
        ],
        compiler_params=pltpu.CompilerParams(vmem_limit_bytes=56 * MIB),
    )(query_weight, key_weight, value_weight, output_weight, dec_input, cotangent, enc_output)
    acc_shape = shape_of((4, tokens, width), F32)
    stack_shape = shape_of((8, feat, 4 * width))

    def begin(pieces, own_group):
        normed, masked, encoded, inv_rms = call(
            prepare_kernel, pieces,
            [
                shape_of((NB, tokens, feat)), shape_of((NB, tokens, feat)),
                shape_of((NB, keys, feat)), shape_of((tokens, 128), F32),
            ],
            (dec_lengths,), moved=12 * MIB,
        )
        acc, own_stack = call(
            own_kernel, (normed, masked, encoded, *own_group), [acc_shape, stack_shape],
            flops=16 * unit, moved=4 * MIB,
        )
        return normed, masked, encoded, inv_rms, own_stack, acc

    near_group, far_group, start = gather(weights, acts, begin)
    normed, masked, encoded, inv_rms, own_stack, acc = start
    stacked = (normed, masked, encoded)
    acc, near_stack = call(
        near_kernel, (*stacked, *near_group, acc), [acc_shape, stack_shape],
        flops=32 * unit, moved=8 * MIB,
    )
    kshape = shape_of((keys, 2 * width))
    kv_grad, q_t, kv_t, at_t, stat, even_stack = call(
        functools.partial(far_kernel, scale), (*stacked, *far_group, acc, own_stack),
        [
            kshape, shape_of((width, tokens)), shape_of((2 * width, keys)),
            shape_of((width, tokens)), shape_of((EXTRA, tokens)), stack_shape,
        ],
        (enc_lengths,), flops=24 * unit, moved=4 * MIB, aliases=((10, 5),),
    )

    def grads(dz, others):
        (normed_in,) = after((normed,), *others) if others else (normed,)
        full, part = shape_of((4 * width, feat)), shape_of((2 * width, feat))
        outs = [full, full, part, part, full] if dz == 2 else [full] * 4
        return call(
            functools.partial(weight_grad_kernel, dz), (normed_in, masked, encoded, q_t, kv_t, at_t),
            outs, scratch=[pltpu.VMEM((4 * width, feat), BF)], flops=16 * unit, moved=4 * MIB,
        )

    def partials(side):
        out = shape_of((2, 4, 3 * tokens + EXTRA, feat))
        return call(
            functools.partial(partial_kernel, side),
            (q_t, kv_grad, at_t, stat, even_stack, near_stack),
            [out], scratch=[pltpu.VMEM((keys // 2, 2 * width), BF)], flops=32 * unit, moved=14 * MIB,
        )[0]

    shares, terms = scatter(grads, partials)
    query_grad, key_grad, value_grad, output_grad = call_out(
        share_kernel, shares, [shape_of((feat, width))] * 4
    )
    stack = shape_of((1, tokens, feat))
    layer_out, input_grad, enc_grad = call_out(
        last_kernel, (*terms, acts, inv_rms),
        [stack, stack, shape_of((1, erows, NB * feat))], (dec_lengths,),
    )
    return (layer_out, input_grad, enc_grad, query_grad, key_grad, value_grad, output_grad)


def solution(mesh):
    in_specs = (
        P("dp", None, "mp"),
        P("dp", "mp", None),
        P("dp", "mp"),
        P("dp", "mp"),
        P("dp", "mp"),
        P("mp", "dp"),
        P("dp", None, "mp"),
        P("dp"),
        P("dp"),
    )
    out_specs = (
        P("dp", None, "mp"),
        P("dp", None, "mp"),
        P("dp", "mp", None),
        P("dp", "mp"),
        P("dp", "mp"),
        P("dp", "mp"),
        P("mp", "dp"),
    )
    return jax.shard_map(local, mesh=mesh, in_specs=in_specs, out_specs=out_specs, check_vma=False)
```

```python
import functools

import jax
import jax.numpy as jnp
from jax import lax
from jax.experimental import pallas as pl
from jax.experimental.pallas import tpu as pltpu
from jax.sharding import PartitionSpec as P

BF = jnp.bfloat16
F32 = jnp.float32
NB = 16
MIB = 1024 * 1024
COST = 4
EXTRA = 16

YZ = [(y, z) for y in range(4) for z in range(4)]
ZXC = [(a, b, c) for a in range(2) for b in range(4) for c in range(2)]


def dp_index(y, z):
    return (y % 4) * 4 + (z % 4)


def mp_index(a, b, c):
    return (a % 2) * 8 + (b % 4) * 2 + (c % 2)


def send_y(value, d):
    return lax.ppermute(value, "dp", [(dp_index(y, z), dp_index(y + d, z)) for y, z in YZ])


def send_z(value, d):
    return lax.ppermute(value, "dp", [(dp_index(y, z), dp_index(y, z + d)) for y, z in YZ])


def send_mp(value, da, db, dc):
    pairs = [(mp_index(a, b, c), mp_index(a + da, b + db, c + dc)) for a, b, c in ZXC]
    return lax.ppermute(value, "mp", pairs)


def send_x(value, bits):
    pairs = [(mp_index(a, b, c), mp_index(a, b ^ bits, c)) for a, b, c in ZXC]
    return lax.ppermute(value, "mp", pairs)


def nn(a, b):
    return lax.dot_general(a, b, (((1,), (0,)), ((), ())), preferred_element_type=F32)


def nt(a, b):
    return lax.dot_general(a, b, (((1,), (1,)), ((), ())), preferred_element_type=F32)


def tn(a, b):
    return lax.dot_general(a, b, (((0,), (0,)), ((), ())), preferred_element_type=F32)


def shape_of(shape, dtype=BF):
    return jax.ShapeDtypeStruct(shape, dtype)


def call(kernel, args, outs, scalars=(), scratch=(), flops=0, moved=0, vmem=8, aliases=()):
    spec = pl.BlockSpec(memory_space=pltpu.VMEM)
    return pl.pallas_call(
        kernel,
        in_specs=[pl.BlockSpec(memory_space=pltpu.SMEM)] * len(scalars) + [spec] * len(args),
        out_specs=[spec] * len(outs),
        out_shape=outs,
        scratch_shapes=scratch,
        input_output_aliases=dict(aliases),
        compiler_params=pltpu.CompilerParams(vmem_limit_bytes=vmem * MIB),
        cost_estimate=pl.CostEstimate(flops=COST * flops, bytes_accessed=moved, transcendentals=0),
    )(*scalars, *args)


def call_out(kernel, args, outs, scalars=()):
    spec = pl.BlockSpec(memory_space=pltpu.VMEM)
    n = len(outs)

    def body(*refs):
        ins, results, sems = refs[: -2 * n - 1], refs[-2 * n - 1 : -n - 1], refs[-1]
        held = refs[-n - 1 : -1]
        kernel(*ins, *held)
        copies = [
            pltpu.make_async_copy(a, b, sems.at[k]) for k, (a, b) in enumerate(zip(held, results))
        ]
        for copy in copies:
            copy.start()
        for copy in copies:
            copy.wait()

    return pl.pallas_call(
        body,
        in_specs=[pl.BlockSpec(memory_space=pltpu.SMEM)] * len(scalars) + [spec] * len(args),
        out_specs=[pl.BlockSpec(memory_space=pltpu.HBM)] * n,
        out_shape=outs,
        scratch_shapes=[pltpu.VMEM(o.shape, o.dtype) for o in outs] + [pltpu.SemaphoreType.DMA((n,))],
        compiler_params=pltpu.CompilerParams(vmem_limit_bytes=8 * MIB),
    )(*scalars, *args)


def mp_place():
    place = lax.axis_index("mp")
    return lax.div(place, 8), lax.rem(lax.div(place, 2), 4), lax.rem(place, 2)


def dp_block(dy, dz):
    part = lax.axis_index("dp")
    return lax.rem(lax.div(part, 4) + dy, 4) * 4 + lax.rem(lax.rem(part, 4) + dz, 4)


def blocks_at(dz):
    return [dp_block(dy, dz) for dy in range(4)]


def after(values, *others):
    out = lax.optimization_barrier((others, tuple(values)))
    return out[1]


def pack_stat(row, shape):
    high = row.astype(BF).astype(F32)
    line = lax.broadcasted_iota(jnp.int32, shape, 0)
    rows = jnp.where(line == 0, high, jnp.where(line == 1, row - high, 0.0))
    return rows.astype(BF)


def stat_of(rows):
    return jnp.sum(rows.astype(F32), axis=0, keepdims=True)


def assemble_kernel(q_ref, k_ref, v_ref, o_ref, dec_ref, cot_ref, enc_ref, block_ref, acts_ref, o_buf, enc_buf, sems):
    width, feat = q_ref.shape[1], cot_ref.shape[2]
    tokens, erows = cot_ref.shape[1], enc_ref.shape[1]
    pairs = [(ref, block_ref.at[:, n * width : (n + 1) * width]) for n, ref in enumerate((q_ref, k_ref, v_ref))]
    pairs += [(o_ref, o_buf), (enc_ref.at[0], enc_buf)]
    pairs += [(dec_ref.at[0], acts_ref.at[:tokens]), (cot_ref.at[0], acts_ref.at[tokens : 2 * tokens])]
    copies = [pltpu.make_async_copy(a, b, sems.at[n]) for n, (a, b) in enumerate(pairs)]
    for copy in copies:
        copy.start()
    copies[3].wait()
    block_ref[:, 3 * width :] = o_buf[...].T
    copies[4].wait()
    for n in range(NB):
        line = 2 * tokens + n * erows
        acts_ref[line : line + erows] = enc_buf[:, n * feat : (n + 1) * feat]
    for n in (0, 1, 2, 5, 6):
        copies[n].wait()


def pair_kernel(first, second, out_ref):
    out_ref[0] = first[...]
    out_ref[1] = second[...]


def pick_kernel(first, second, out_first, out_second):
    out_first[...] = first[0]
    out_second[...] = second[1]


def join_kernel(first, second, out_ref):
    half = first.shape[0]
    out_ref[:half] = first[...]
    out_ref[half:] = second[...]


def halves_kernel(first, second, out_first, out_second):
    half = out_first.shape[0]
    out_first[...] = first[:half]
    out_second[...] = second[half:]


def quad_kernel(*refs):
    for n, ref in enumerate(refs[:4]):
        refs[4][n] = ref[...]


def prepare_kernel(len_ref, own_ref, other_ref, normed_ref, masked_ref, enc_ref, inv_ref):
    tokens, feat = normed_ref.shape[1:]
    erows = enc_ref.shape[1] // NB
    a, b, c = mp_place()
    square = jnp.zeros((tokens, 1), F32)
    for piece in (own_ref, other_ref):

        def add_squares(k, total, piece=piece):
            hidden = piece[lax.div(k, 4), lax.rem(k, 4), :tokens].astype(F32)
            return total + jnp.sum(hidden * hidden, axis=1, keepdims=True)

        square = lax.fori_loop(0, 8, add_squares, square)
    inv_rms = lax.rsqrt(square / (NB * feat) + 1e-06)
    inv_ref[...] = jnp.broadcast_to(inv_rms, inv_ref.shape)
    keep = lax.broadcasted_iota(jnp.int32, (tokens, feat), 0) < len_ref[0]
    for n, piece in enumerate((own_ref, other_ref)):

        def write(k, carry, n=n, piece=piece):
            z, x = lax.div(k, 4), lax.rem(k, 4)
            place = lax.rem(a + z, 2) * 8 + lax.rem(b + 4 - x, 4) * 2 + lax.rem(c + n, 2)
            normed_ref[place] = (piece[z, x, :tokens].astype(F32) * inv_ref[:, :1]).astype(BF)
            rows = piece[z, x, tokens : 2 * tokens]
            masked_ref[place] = jnp.where(keep, rows.astype(F32), 0.0).astype(BF)
            start = pl.multiple_of(place * erows, erows)
            for m in range(NB):
                line = 2 * tokens + m * erows
                enc_ref[m, pl.ds(start, erows), :] = piece[z, x, line : line + erows]
            return carry

        lax.fori_loop(0, 8, write, 0)


def attention(scale, enc_len, query, keyed, valued, attended_grad):
    scores = nt(query, keyed) * scale
    column = lax.broadcasted_iota(jnp.int32, scores.shape, 1)
    scores = jnp.where(column < enc_len, scores, -1e30)
    shifted = jnp.exp(scores - jnp.max(scores, axis=-1, keepdims=True))
    probs = shifted / jnp.sum(shifted, axis=-1, keepdims=True)
    probs_low = probs.astype(BF)
    attended = nn(probs_low, valued).astype(BF)
    probs_grad = nt(attended_grad, valued)
    inner = jnp.sum(probs * probs_grad, axis=-1, keepdims=True)
    scores_grad = (probs * (probs_grad - inner) * scale).astype(BF)
    q_grad = nn(scores_grad, keyed).astype(BF)
    k_grad = tn(scores_grad, query).astype(BF)
    v_grad = tn(probs_low, attended_grad).astype(BF)
    stat = jnp.sum(q_grad.astype(F32) * query.astype(F32), axis=-1, keepdims=True)
    return q_grad, k_grad, v_grad, attended, stat


def project(places, pieces, normed_ref, masked_ref, enc_ref, stack_ref, init, first=0):
    width = stack_ref.shape[2] // 4
    for n, piece in enumerate(pieces):
        stack_ref[first + n] = piece()
    out = init
    for n in range(0, len(pieces), 4):
        group = places[n : n + 4]
        rows = jnp.concatenate([stack_ref[first + n + k] for k in range(4)], axis=0)
        normed, enc, masked = (
            jnp.concatenate([ref[p] for p in group], axis=1)
            for ref in (normed_ref, enc_ref, masked_ref)
        )
        new = (
            nn(normed, rows[:, :width]),
            nn(enc, rows[:, width : 2 * width]),
            nn(enc, rows[:, 2 * width : 3 * width]),
            nn(masked, rows[:, 3 * width :]),
        )
        out = new if out is None else tuple(o + v for o, v in zip(out, new))
    return out


def one(ref):
    return lambda: ref[...]


def at(ref, n):
    return lambda: ref[n]


def both(low, high):
    return lambda: jnp.concatenate([low[...], high[...]], axis=0)


def own_kernel(normed_ref, masked_ref, enc_ref, *refs):
    own, high, low, across, acc_ref, stack_ref = refs
    pieces = [one(own), one(high), one(across), one(low)]
    acc = project(blocks_at(0), pieces, normed_ref, masked_ref, enc_ref, stack_ref, None)
    for n in range(4):
        acc_ref[n] = acc[n]


def near_kernel(normed_ref, masked_ref, enc_ref, *refs):
    pair, high, low, across_b, across_a, acc_in, acc_ref, stack_ref = refs
    pieces = [at(pair, 0), at(high, 0), one(across_b), at(low, 0)]
    pieces += [at(pair, 1), at(high, 1), one(across_a), at(low, 1)]
    width = stack_ref.shape[2] // 4
    for n, piece in enumerate(pieces):
        stack_ref[n] = piece()
    for n in range(4):
        acc_ref[n] = acc_in[n]

    def body(group, carry):
        places = [dp_block(dy, 3 - 2 * group) for dy in range(4)]
        rows = jnp.concatenate([stack_ref[4 * group + k] for k in range(4)], axis=0)
        normed, enc, masked = (
            jnp.concatenate([ref[p] for p in places], axis=1)
            for ref in (normed_ref, enc_ref, masked_ref)
        )
        for n, left in enumerate((normed, enc, enc, masked)):
            acc_ref[n] += nn(left, rows[:, n * width : (n + 1) * width])
        return carry

    lax.fori_loop(0, 2, body, 0)


def far_kernel(scale, len_ref, normed_ref, masked_ref, enc_ref, *refs):
    far, high, low, across_low, across_high, acc_in = refs[:6]
    kv_ref, qgt_ref, kvt_ref, att_ref, stat_ref, stack_ref = refs[7:]
    pieces = [one(far), one(high), both(across_low, across_high), one(low)]
    init = [acc_in[n] for n in range(4)]
    acc = project(blocks_at(2), pieces, normed_ref, masked_ref, enc_ref, stack_ref, init, 4)
    out = attention(scale, len_ref[0], *(value.astype(BF) for value in acc))
    q_grad, k_grad, v_grad, attended, stat = out
    width = q_grad.shape[1]
    kv_ref[:, :width] = k_grad
    kv_ref[:, width:] = v_grad
    qgt_ref[...] = q_grad.T
    kvt_ref[:width] = k_grad.T
    kvt_ref[width:] = v_grad.T
    att_ref[...] = attended.T
    row = jnp.broadcast_to(stat, (stat.shape[0], 128)).T[0:1]
    stat_ref[...] = pack_stat(row, stat_ref.shape)


def weight_grad_kernel(dz, normed_ref, masked_ref, enc_ref, *refs):
    qgt_ref, kvt_ref, att_ref = refs[:3]
    outs, held = refs[3:-1], refs[-1]
    width = qgt_ref.shape[0]
    targets = [outs[0], outs[1], outs[2:-1], outs[-1]]

    def body(n, carry):
        place = dp_block(n, dz)
        held[:width] = nn(qgt_ref[...], normed_ref[place]).astype(BF)
        held[width : 3 * width] = nn(kvt_ref[...], enc_ref[place]).astype(BF)
        held[3 * width :] = nn(att_ref[...], masked_ref[place]).astype(BF)
        for k, target in enumerate(targets):

            @pl.when(n == k)
            def _():
                parts = target if isinstance(target, tuple) else (target,)
                first = 0
                for part in parts:
                    part[...] = held[first : first + part.shape[0]]
                    first += part.shape[0]

        return carry

    lax.fori_loop(0, 4, body, 0)


def partial_kernel(side, q_t_ref, kv_ref, at_t_ref, stat_ref, even, odd, out, kv_buf):
    width, tokens = q_t_ref.shape
    erows = kv_ref.shape[0] // NB
    a, b, c = mp_place()
    core = lax.rem(c + side, 2)
    for x in range(4):
        for z in range(2):
            out[z, x, 3 * tokens :, :] = stat_ref[...]
            owner = lax.rem(a + z, 2) * 8 + lax.bitwise_xor(b, x) * 2 + core
            start = pl.multiple_of(owner * erows, erows)
            line = (x * 2 + z) * erows
            kv_buf[line : line + erows, :] = kv_ref[pl.ds(start, erows), :]

    def block_of(n, shifts):
        return dp_block(lax.rem(n, 4), jnp.where(n < 4, shifts[0], shifts[1]))

    stacks = ((even, (0, 2)), (odd, (3, 1)))
    for stack, shifts in stacks:

        def enc_part(n, carry, stack=stack, shifts=shifts):
            line = pl.multiple_of(2 * tokens + block_of(n, shifts) * erows, erows)
            enc = nt(kv_buf[...], stack[n, :, width : 3 * width]).astype(BF)
            for x in range(4):
                for z in range(2):
                    first = (x * 2 + z) * erows
                    out[z, x, pl.ds(line, erows), :] = enc[first : first + erows]
            return carry

        lax.fori_loop(0, stack.shape[0], enc_part, 0, unroll=2)

    last = lax.rem(lax.axis_index("dp") + core, 2)
    for stack, shifts in stacks:

        @pl.when(last == shifts[0] % 2)
        def _():
            def parts(n, carry):
                place = block_of(n, shifts)
                xr = lax.bitwise_xor(lax.rem(lax.div(place, 2), 4), b)
                zr = lax.rem(lax.div(place, 8) + 2 - a, 2)
                out[zr, xr, :tokens, :] = nn(stack[n, :, :width], q_t_ref[...]).astype(BF)
                out_part = nn(stack[n, :, 3 * width :], at_t_ref[...]).astype(BF)
                out[zr, xr, tokens : 2 * tokens, :] = out_part
                return carry

            lax.fori_loop(0, stack.shape[0], parts, 0, unroll=2)


def add_rows(ins, out):
    rows, feat = out.shape[0] - EXTRA, out.shape[1]

    def body(step, carry):
        part = pl.ds(pl.multiple_of(step * CHUNK, CHUNK), CHUNK)
        total = ins[0][part, :].astype(F32)
        for ref in ins[1:]:
            total += ref[part, :].astype(F32)
        out[part, :] = total.astype(BF)
        return carry

    lax.fori_loop(0, rows // CHUNK, body, 0)
    stat = stat_of(ins[0][rows:])
    for ref in ins[1:]:
        stat += stat_of(ref[rows:])
    out[rows:] = pack_stat(stat, (EXTRA, feat))


def core_sum_kernel(keep_ref, got_ref, *outs):
    for z, out in enumerate(outs):

        def body(x, carry, z=z, out=out):
            add_rows([keep_ref.at[z, x], got_ref.at[z, x]], out.at[x])
            return carry

        lax.fori_loop(0, 4, body, 0)


def z_sum_kernel(keep_ref, got_ref, *outs):
    for n, out in enumerate(outs):

        def body(x, carry, n=n, out=out):
            add_rows([keep_ref.at[2 * n + x], got_ref.at[2 * n + x]], out.at[x])
            return carry

        lax.fori_loop(0, 2, body, 0)


def x_sum_kernel(first_ref, second_ref, *outs):
    for n, out in enumerate(outs):
        add_rows([first_ref.at[n], second_ref.at[n]], out)


def share_kernel(*refs):
    ins, outs = refs[:-4], refs[-4:]
    total = ins[0][...].astype(F32)
    for ref in ins[1:]:
        total += ref[...].astype(F32)
    total = total.astype(BF)
    width = outs[0].shape[1]
    for n, out in enumerate(outs[:3]):
        out[...] = total[n * width : (n + 1) * width].T
    outs[3][...] = total[3 * width :]


def last_kernel(len_ref, *refs):
    terms, (acts_ref, inv_ref, out_ref, in_ref, enc_ref) = refs[:2], refs[2:]
    tokens, feat = out_ref.shape[1:]
    rows = 3 * tokens
    total = [sum(ref[n * tokens : (n + 1) * tokens].astype(F32) for ref in terms) for n in range(3)]
    total[0], total[1] = total[0].T, total[1].T
    stat = sum(stat_of(ref[rows:]) for ref in terms)
    stat = jnp.broadcast_to(stat, (128, tokens)).T[:, :1] / (NB * feat)
    inv_rms = inv_ref[:, :1]
    dec = acts_ref[:tokens].astype(F32)
    out_ref[0] = (dec + total[1]).astype(BF)
    keep = lax.broadcasted_iota(jnp.int32, (tokens, feat), 0) < len_ref[0]
    masked = jnp.where(keep, acts_ref[tokens : 2 * tokens].astype(F32), 0.0)
    in_grad = masked + inv_rms * total[0] - dec * (inv_rms * inv_rms * stat)
    in_ref[0] = in_grad.astype(BF)
    erows = enc_ref.shape[1]
    for n in range(NB):
        enc_ref[0, :, n * feat : (n + 1) * feat] = total[2][n * erows : (n + 1) * erows].astype(BF)


def stack_pair(first, second):
    return call(pair_kernel, (first, second), [shape_of((2,) + first.shape)])[0]


def halves(first, second):
    half = shape_of((first.shape[0] // 2, first.shape[1]))
    return call(halves_kernel, (first, second), [half] * 2)


def gather(block, acts, begin):
    x3 = send_mp(acts, 0, 3, 0)
    before, behind = send_z(block, 1), send_z(block, -1)
    low, high = send_y(block, 1), send_y(block, -1)
    x3, to_x, again = after((x3, acts, block), low, high)
    x1, x2 = send_mp(to_x, 0, 1, 0), send_mp(to_x, 0, 2, 0)
    across = send_y(again, 2)

    x1, x2, x3, before, behind = after((x1, x2, x3, before, behind), across)
    (quad,) = call(quad_kernel, (acts, x1, x2, x3), [shape_of((4,) + acts.shape)])
    pair = stack_pair(before, behind)
    pair_low, pair_high = send_y(pair, 1), send_y(pair, -1)
    to_low, to_high = halves(before, behind)
    far_low, far_high = send_z(to_low, 1), send_z(to_high, -1)
    (to_other,) = after((quad,), far_low, far_high)
    other = send_mp(to_other, 1, 0, 0)

    pair_low, pair_high, far_low, far_high = after((pair_low, pair_high, far_low, far_high))
    (far,) = call(join_kernel, (far_low, far_high), [shape_of(block.shape)])
    f_low, f_high = send_y(far, 1), send_y(far, -1)
    to_low, to_high = call(pick_kernel, (pair_low, pair_high), [shape_of(block.shape)] * 2)
    across_b, across_a = send_y(to_low, 1), send_y(to_high, -1)

    quad, other, f_low, f_high = after((quad, other, f_low, f_high), across_a, across_b)
    (line,) = call(pair_kernel, (quad, other), [shape_of((2,) + quad.shape)])
    sibling = send_mp(line, 0, 0, 1)
    to_low, to_high = halves(f_low, f_high)
    last_low, last_high = send_y(to_low, 1), send_y(to_high, -1)
    return (
        (pair, pair_high, pair_low, across_b, across_a),
        (far, f_high, f_low, last_low, last_high),
        begin((line, sibling), (block, high, low, across)),
    )


CHUNK = 128


def summed(out, put, *terms):
    def body(step, carry):
        rows = pl.ds(pl.multiple_of(step * CHUNK, CHUNK), CHUNK)
        total = terms[0](rows).astype(F32)
        for term in terms[1:]:
            total += term(rows).astype(F32)
        put(out, rows, total.astype(BF))
        return carry

    lax.fori_loop(0, out.shape[-2] // CHUNK, body, 0)


def plain(ref):
    return lambda rows: ref[rows, :]


def of(ref, n):
    return lambda rows: ref[n, rows, :]


def put_plain(out, rows, value):
    out[rows, :] = value


def put_at(n):
    def put(out, rows, value):
        out[n, rows, :] = value

    return put


def far_kernel_sum(far1, far3, low, high, out1, out3):
    half = low.shape[0]
    for ref, part, out, first in ((far1, low, out1, 0), (far3, high, out3, half)):
        rest = slice(half - first, 2 * half - first)
        out[rest] = ref[rest]
        here = ref.at[first : first + half]
        summed(out.at[first : first + half], put_plain, plain(here), plain(part))


def second_sum_kernel(far0, far1, far3, bf1, bf2, bf3, bh1, bh2, bh3, up, down, far_low, far_high):
    summed(up, put_at(0), plain(bf1), plain(bf2))
    summed(up, put_at(1), plain(bh1))
    summed(down, put_at(0), plain(bf3))
    summed(down, put_at(1), plain(bh3), plain(bh2))
    half = far_low.shape[0]
    for out, first in ((far_low, 0), (far_high, half)):
        summed(out, put_plain, *(plain(ref.at[first : first + half]) for ref in (far0, far1, far3)))


def third_sum_kernel(bf0, bh0, up, down, low, high, before, behind):
    half = low.shape[0]
    for out, ref, n, part, first in ((before, bf0, 0, low, 0), (behind, bh0, 1, high, half)):

        def body(step, carry, out=out, ref=ref, n=n, part=part, first=first):
            begin = pl.multiple_of(step * CHUNK, CHUNK)
            rows, here = pl.ds(begin + first, CHUNK), pl.ds(begin, CHUNK)
            rest = pl.ds(begin + half - first, CHUNK)
            total = ref[rows, :].astype(F32) + up[n, rows, :].astype(F32)
            total += down[n, rows, :].astype(F32) + part[here, :].astype(F32)
            out[rows, :] = total.astype(BF)
            total = ref[rest, :].astype(F32) + up[n, rest, :].astype(F32)
            total += down[n, rest, :].astype(F32)
            out[rest, :] = total.astype(BF)
            return carry

        lax.fori_loop(0, half // CHUNK, body, 0)


def scatter(grads, partials):
    send = partials(1)
    core = send_mp(send, 0, 0, 1)
    far0, far1, far2_low, far2_high, far3 = grads(2, (send,))
    full = shape_of(far0.shape)
    pair = shape_of((2,) + far0.shape)
    far2_low, far2_high = send_y(far2_low, 1), send_y(far2_high, -1)
    bf0, bf1, bf2, bf3 = grads(1, (far0,))
    bh0, bh1, bh2, bh3 = grads(3, (bf0,))
    keep = partials(0)

    core, keep, far2_low, far2_high, bf2, bh2 = after(
        (core, keep, far2_low, far2_high, bf2, bh2)
    )
    own0, own1, own2, own3 = grads(0, (core,))
    part = shape_of(keep.shape[1:])
    own_z, other_z = call(core_sum_kernel, (keep, core), [part] * 2, moved=9 * MIB)
    other_z = send_mp(other_z, 1, 0, 0)
    bf2, bh2 = send_y(bf2, 1), send_y(bh2, -1)
    far1, far3 = call(far_kernel_sum, (far1, far3, far2_low, far2_high), [full] * 2)
    far1, far3 = send_y(far1, 1), send_y(far3, -1)

    far1, far3, bf2, bh2 = after((far1, far3, bf2, bh2))
    half = shape_of(far2_low.shape)
    up, down, far_low, far_high = call(
        second_sum_kernel, (far0, far1, far3, bf1, bf2, bf3, bh1, bh2, bh3),
        [pair, pair, half, half],
    )
    up, down = send_y(up, 1), send_y(down, -1)
    far_low, far_high = send_z(far_low, 1), send_z(far_high, -1)
    (other_z,) = after((other_z,), far_low, far_high)
    part = shape_of((2,) + keep.shape[2:])
    near_x, far_x = call(z_sum_kernel, (own_z, other_z), [part] * 2, moved=6 * MIB)
    far_x = send_x(far_x, 2)

    up, down, far_low, far_high, own1, own2, own3 = after(
        (up, down, far_low, far_high, own1, own2, own3)
    )
    before, behind = call(
        third_sum_kernel, (bf0, bh0, up, down, far_low, far_high), [full] * 2
    )
    before, behind = send_z(before, 1), send_z(behind, -1)
    own1, own3 = send_y(own1, 1), send_y(own3, -1)
    own2, own1, own3 = after((own2, own1, own3))
    own2 = send_y(own2, 2)
    part = shape_of(keep.shape[2:])
    own_x, next_x = call(x_sum_kernel, (near_x, far_x), [part] * 2, moved=3 * MIB)
    return (own0, own1, own2, own3, before, behind), (own_x, send_x(next_x, 1))


def local(
    dec_input,
    enc_output,
    query_weight,
    key_weight,
    value_weight,
    output_weight,
    cotangent,
    enc_lengths,
    dec_lengths,
):
    tokens, feat = dec_input.shape[1:]
    width = query_weight.shape[1]
    erows = enc_output.shape[1]
    keys = erows * NB
    scale = width ** (-0.5)
    unit = 2 * tokens * feat * width

    hbm = pl.BlockSpec(memory_space=pltpu.HBM)
    vmem = pl.BlockSpec(memory_space=pltpu.VMEM)
    weights, acts = pl.pallas_call(
        assemble_kernel,
        in_specs=[hbm] * 7,
        out_specs=[vmem] * 2,
        out_shape=[shape_of((feat, 4 * width)), shape_of((2 * tokens + keys, feat))],
        scratch_shapes=[
            pltpu.VMEM((width, feat), BF), pltpu.VMEM((erows, NB * feat), BF),
            pltpu.SemaphoreType.DMA((7,)),
        ],
        compiler_params=pltpu.CompilerParams(vmem_limit_bytes=56 * MIB),
    )(query_weight, key_weight, value_weight, output_weight, dec_input, cotangent, enc_output)
    acc_shape = shape_of((4, tokens, width), F32)
    stack_shape = shape_of((8, feat, 4 * width))

    def begin(pieces, own_group):
        normed, masked, encoded, inv_rms = call(
            prepare_kernel, pieces,
            [
                shape_of((NB, tokens, feat)), shape_of((NB, tokens, feat)),
                shape_of((NB, keys, feat)), shape_of((tokens, 128), F32),
            ],
            (dec_lengths,), moved=12 * MIB,
        )
        acc, own_stack = call(
            own_kernel, (normed, masked, encoded, *own_group), [acc_shape, stack_shape],
            flops=16 * unit, moved=4 * MIB,
        )
        return normed, masked, encoded, inv_rms, own_stack, acc

    near_group, far_group, start = gather(weights, acts, begin)
    normed, masked, encoded, inv_rms, own_stack, acc = start
    stacked = (normed, masked, encoded)
    acc, near_stack = call(
        near_kernel, (*stacked, *near_group, acc), [acc_shape, stack_shape],
        flops=32 * unit, moved=8 * MIB,
    )
    kshape = shape_of((keys, 2 * width))
    kv_grad, q_t, kv_t, at_t, stat, even_stack = call(
        functools.partial(far_kernel, scale), (*stacked, *far_group, acc, own_stack),
        [
            kshape, shape_of((width, tokens)), shape_of((2 * width, keys)),
            shape_of((width, tokens)), shape_of((EXTRA, tokens)), stack_shape,
        ],
        (enc_lengths,), flops=24 * unit, moved=4 * MIB, aliases=((10, 5),),
    )

    def grads(dz, others):
        (normed_in,) = after((normed,), *others) if others else (normed,)
        full, part = shape_of((4 * width, feat)), shape_of((2 * width, feat))
        outs = [full, full, part, part, full] if dz == 2 else [full] * 4
        return call(
            functools.partial(weight_grad_kernel, dz), (normed_in, masked, encoded, q_t, kv_t, at_t),
            outs, scratch=[pltpu.VMEM((4 * width, feat), BF)], flops=16 * unit, moved=4 * MIB,
        )

    def partials(side):
        out = shape_of((2, 4, 3 * tokens + EXTRA, feat))
        return call(
            functools.partial(partial_kernel, side),
            (q_t, kv_grad, at_t, stat, even_stack, near_stack),
            [out], scratch=[pltpu.VMEM((keys // 2, 2 * width), BF)], flops=32 * unit, moved=14 * MIB,
        )[0]

    shares, terms = scatter(grads, partials)
    query_grad, key_grad, value_grad, output_grad = call_out(
        share_kernel, shares, [shape_of((feat, width))] * 4
    )
    stack = shape_of((1, tokens, feat))
    layer_out, input_grad, enc_grad = call_out(
        last_kernel, (*terms, acts, inv_rms),
        [stack, stack, shape_of((1, erows, NB * feat))], (dec_lengths,),
    )
    return (layer_out, input_grad, enc_grad, query_grad, key_grad, value_grad, output_grad)


def solution(mesh):
    in_specs = (
        P("dp", None, "mp"),
        P("dp", "mp", None),
        P("dp", "mp"),
        P("dp", "mp"),
        P("dp", "mp"),
        P("mp", "dp"),
        P("dp", None, "mp"),
        P("dp"),
        P("dp"),
    )
    out_specs = (
        P("dp", None, "mp"),
        P("dp", None, "mp"),
        P("dp", "mp", None),
        P("dp", "mp"),
        P("dp", "mp"),
        P("dp", "mp"),
        P("mp", "dp"),
    )
    return jax.shard_map(local, mesh=mesh, in_specs=in_specs, out_specs=out_specs, check_vma=False)
```

```python
import functools

import jax
import jax.numpy as jnp
from jax import lax
from jax.experimental import pallas as pl
from jax.experimental.pallas import tpu as pltpu
from jax.sharding import PartitionSpec as P

BF = jnp.bfloat16
F32 = jnp.float32
NB = 16
MIB = 1024 * 1024
COST = 4
EXTRA = 16

YZ = [(y, z) for y in range(4) for z in range(4)]
ZXC = [(a, b, c) for a in range(2) for b in range(4) for c in range(2)]


def dp_index(y, z):
    return (y % 4) * 4 + (z % 4)


def mp_index(a, b, c):
    return (a % 2) * 8 + (b % 4) * 2 + (c % 2)


def send_y(value, d):
    return lax.ppermute(value, "dp", [(dp_index(y, z), dp_index(y + d, z)) for y, z in YZ])


def send_z(value, d):
    return lax.ppermute(value, "dp", [(dp_index(y, z), dp_index(y, z + d)) for y, z in YZ])


def send_mp(value, da, db, dc):
    pairs = [(mp_index(a, b, c), mp_index(a + da, b + db, c + dc)) for a, b, c in ZXC]
    return lax.ppermute(value, "mp", pairs)


def send_x(value, bits):
    pairs = [(mp_index(a, b, c), mp_index(a, b ^ bits, c)) for a, b, c in ZXC]
    return lax.ppermute(value, "mp", pairs)


def nn(a, b):
    return lax.dot_general(a, b, (((1,), (0,)), ((), ())), preferred_element_type=F32)


def nt(a, b):
    return lax.dot_general(a, b, (((1,), (1,)), ((), ())), preferred_element_type=F32)


def tn(a, b):
    return lax.dot_general(a, b, (((0,), (0,)), ((), ())), preferred_element_type=F32)


def shape_of(shape, dtype=BF):
    return jax.ShapeDtypeStruct(shape, dtype)


def call(kernel, args, outs, scalars=(), scratch=(), flops=0, moved=0, vmem=8, aliases=()):
    spec = pl.BlockSpec(memory_space=pltpu.VMEM)
    return pl.pallas_call(
        kernel,
        in_specs=[pl.BlockSpec(memory_space=pltpu.SMEM)] * len(scalars) + [spec] * len(args),
        out_specs=[spec] * len(outs),
        out_shape=outs,
        scratch_shapes=scratch,
        input_output_aliases=dict(aliases),
        compiler_params=pltpu.CompilerParams(vmem_limit_bytes=vmem * MIB),
        cost_estimate=pl.CostEstimate(flops=COST * flops, bytes_accessed=moved, transcendentals=0),
    )(*scalars, *args)


def call_out(kernel, args, outs, scalars=()):
    spec = pl.BlockSpec(memory_space=pltpu.VMEM)
    n = len(outs)

    def body(*refs):
        ins, results, sems = refs[: -2 * n - 1], refs[-2 * n - 1 : -n - 1], refs[-1]
        held = refs[-n - 1 : -1]
        kernel(*ins, *held)
        copies = [
            pltpu.make_async_copy(a, b, sems.at[k]) for k, (a, b) in enumerate(zip(held, results))
        ]
        for copy in copies:
            copy.start()
        for copy in copies:
            copy.wait()

    return pl.pallas_call(
        body,
        in_specs=[pl.BlockSpec(memory_space=pltpu.SMEM)] * len(scalars) + [spec] * len(args),
        out_specs=[pl.BlockSpec(memory_space=pltpu.HBM)] * n,
        out_shape=outs,
        scratch_shapes=[pltpu.VMEM(o.shape, o.dtype) for o in outs] + [pltpu.SemaphoreType.DMA((n,))],
        compiler_params=pltpu.CompilerParams(vmem_limit_bytes=8 * MIB),
    )(*scalars, *args)


def mp_place():
    place = lax.axis_index("mp")
    return lax.div(place, 8), lax.rem(lax.div(place, 2), 4), lax.rem(place, 2)


def dp_block(dy, dz):
    part = lax.axis_index("dp")
    return lax.rem(lax.div(part, 4) + dy, 4) * 4 + lax.rem(lax.rem(part, 4) + dz, 4)


def blocks_at(dz):
    return [dp_block(dy, dz) for dy in range(4)]


def after(values, *others):
    out = lax.optimization_barrier((others, tuple(values)))
    return out[1]


def pack_stat(row, shape):
    high = row.astype(BF).astype(F32)
    line = lax.broadcasted_iota(jnp.int32, shape, 0)
    rows = jnp.where(line == 0, high, jnp.where(line == 1, row - high, 0.0))
    return rows.astype(BF)


def stat_of(rows):
    return jnp.sum(rows.astype(F32), axis=0, keepdims=True)


def assemble_kernel(q_ref, k_ref, v_ref, o_ref, dec_ref, cot_ref, enc_ref, block_ref, acts_ref, o_buf, enc_buf, sems):
    width, feat = q_ref.shape[1], cot_ref.shape[2]
    tokens, erows = cot_ref.shape[1], enc_ref.shape[1]
    pairs = [(ref, block_ref.at[:, n * width : (n + 1) * width]) for n, ref in enumerate((q_ref, k_ref, v_ref))]
    pairs += [(o_ref, o_buf), (enc_ref.at[0], enc_buf)]
    pairs += [(dec_ref.at[0], acts_ref.at[:tokens]), (cot_ref.at[0], acts_ref.at[tokens : 2 * tokens])]
    copies = [pltpu.make_async_copy(a, b, sems.at[n]) for n, (a, b) in enumerate(pairs)]
    for copy in copies:
        copy.start()
    copies[3].wait()
    block_ref[:, 3 * width :] = o_buf[...].T
    copies[4].wait()
    for n in range(NB):
        line = 2 * tokens + n * erows
        acts_ref[line : line + erows] = enc_buf[:, n * feat : (n + 1) * feat]
    for n in (0, 1, 2, 5, 6):
        copies[n].wait()


def pair_kernel(first, second, out_ref):
    out_ref[0] = first[...]
    out_ref[1] = second[...]


def pick_kernel(first, second, out_first, out_second):
    out_first[...] = first[0]
    out_second[...] = second[1]


def join_kernel(first, second, out_ref):
    half = first.shape[0]
    out_ref[:half] = first[...]
    out_ref[half:] = second[...]


def halves_kernel(first, second, out_first, out_second):
    half = out_first.shape[0]
    out_first[...] = first[:half]
    out_second[...] = second[half:]


def quad_kernel(*refs):
    for n, ref in enumerate(refs[:4]):
        refs[4][n] = ref[...]


def prepare_kernel(len_ref, own_ref, other_ref, normed_ref, masked_ref, enc_ref, inv_ref):
    tokens, feat = normed_ref.shape[1:]
    erows = enc_ref.shape[1] // NB
    a, b, c = mp_place()
    square = jnp.zeros((tokens, 1), F32)
    for piece in (own_ref, other_ref):

        def add_squares(k, total, piece=piece):
            hidden = piece[lax.div(k, 4), lax.rem(k, 4), :tokens].astype(F32)
            return total + jnp.sum(hidden * hidden, axis=1, keepdims=True)

        square = lax.fori_loop(0, 8, add_squares, square)
    inv_rms = lax.rsqrt(square / (NB * feat) + 1e-06)
    inv_ref[...] = jnp.broadcast_to(inv_rms, inv_ref.shape)
    keep = lax.broadcasted_iota(jnp.int32, (tokens, feat), 0) < len_ref[0]
    for n, piece in enumerate((own_ref, other_ref)):

        def write(k, carry, n=n, piece=piece):
            z, x = lax.div(k, 4), lax.rem(k, 4)
            place = lax.rem(a + z, 2) * 8 + lax.rem(b + 4 - x, 4) * 2 + lax.rem(c + n, 2)
            normed_ref[place] = (piece[z, x, :tokens].astype(F32) * inv_ref[:, :1]).astype(BF)
            rows = piece[z, x, tokens : 2 * tokens]
            masked_ref[place] = jnp.where(keep, rows.astype(F32), 0.0).astype(BF)
            start = pl.multiple_of(place * erows, erows)
            for m in range(NB):
                line = 2 * tokens + m * erows
                enc_ref[m, pl.ds(start, erows), :] = piece[z, x, line : line + erows]
            return carry

        lax.fori_loop(0, 8, write, 0)


def attention(scale, enc_len, query, keyed, valued, attended_grad):
    scores = nt(query, keyed) * scale
    column = lax.broadcasted_iota(jnp.int32, scores.shape, 1)
    scores = jnp.where(column < enc_len, scores, -1e30)
    shifted = jnp.exp(scores - jnp.max(scores, axis=-1, keepdims=True))
    probs = shifted / jnp.sum(shifted, axis=-1, keepdims=True)
    probs_low = probs.astype(BF)
    attended = nn(probs_low, valued).astype(BF)
    probs_grad = nt(attended_grad, valued)
    inner = jnp.sum(probs * probs_grad, axis=-1, keepdims=True)
    scores_grad = (probs * (probs_grad - inner) * scale).astype(BF)
    q_grad = nn(scores_grad, keyed).astype(BF)
    k_grad = tn(scores_grad, query).astype(BF)
    v_grad = tn(probs_low, attended_grad).astype(BF)
    stat = jnp.sum(q_grad.astype(F32) * query.astype(F32), axis=-1, keepdims=True)
    return q_grad, k_grad, v_grad, attended, stat


def project(places, pieces, normed_ref, masked_ref, enc_ref, stack_ref, init, first=0):
    width = stack_ref.shape[2] // 4
    for n, piece in enumerate(pieces):
        stack_ref[first + n] = piece()
    out = init
    for n in range(0, len(pieces), 4):
        group = places[n : n + 4]
        rows = jnp.concatenate([stack_ref[first + n + k] for k in range(4)], axis=0)
        normed, enc, masked = (
            jnp.concatenate([ref[p] for p in group], axis=1)
            for ref in (normed_ref, enc_ref, masked_ref)
        )
        new = (
            nn(normed, rows[:, :width]),
            nn(enc, rows[:, width : 2 * width]),
            nn(enc, rows[:, 2 * width : 3 * width]),
            nn(masked, rows[:, 3 * width :]),
        )
        out = new if out is None else tuple(o + v for o, v in zip(out, new))
    return out


def one(ref):
    return lambda: ref[...]


def at(ref, n):
    return lambda: ref[n]


def both(low, high):
    return lambda: jnp.concatenate([low[...], high[...]], axis=0)


def own_kernel(normed_ref, masked_ref, enc_ref, *refs):
    own, high, low, across, acc_ref, stack_ref = refs
    pieces = [one(own), one(high), one(across), one(low)]
    acc = project(blocks_at(0), pieces, normed_ref, masked_ref, enc_ref, stack_ref, None)
    for n in range(4):
        acc_ref[n] = acc[n]


def near_kernel(normed_ref, masked_ref, enc_ref, *refs):
    pair, high, low, across_b, across_a, acc_in, acc_ref, stack_ref = refs
    pieces = [at(pair, 0), at(high, 0), one(across_b), at(low, 0)]
    pieces += [at(pair, 1), at(high, 1), one(across_a), at(low, 1)]
    width = stack_ref.shape[2] // 4
    for n, piece in enumerate(pieces):
        stack_ref[n] = piece()
    for n in range(4):
        acc_ref[n] = acc_in[n]

    def body(group, carry):
        places = [dp_block(dy, 3 - 2 * group) for dy in range(4)]
        rows = jnp.concatenate([stack_ref[4 * group + k] for k in range(4)], axis=0)
        normed, enc, masked = (
            jnp.concatenate([ref[p] for p in places], axis=1)
            for ref in (normed_ref, enc_ref, masked_ref)
        )
        for n, left in enumerate((normed, enc, enc, masked)):
            acc_ref[n] += nn(left, rows[:, n * width : (n + 1) * width])
        return carry

    lax.fori_loop(0, 2, body, 0)


def far_kernel(scale, len_ref, normed_ref, masked_ref, enc_ref, *refs):
    far, high, low, across_low, across_high, acc_in = refs[:6]
    kv_ref, qgt_ref, kvt_ref, att_ref, stat_ref, stack_ref = refs[7:]
    pieces = [one(far), one(high), both(across_low, across_high), one(low)]
    init = [acc_in[n] for n in range(4)]
    acc = project(blocks_at(2), pieces, normed_ref, masked_ref, enc_ref, stack_ref, init, 4)
    out = attention(scale, len_ref[0], *(value.astype(BF) for value in acc))
    q_grad, k_grad, v_grad, attended, stat = out
    width = q_grad.shape[1]
    kv_ref[:, :width] = k_grad
    kv_ref[:, width:] = v_grad
    qgt_ref[...] = q_grad.T
    kvt_ref[:width] = k_grad.T
    kvt_ref[width:] = v_grad.T
    att_ref[...] = attended.T
    row = jnp.broadcast_to(stat, (stat.shape[0], 128)).T[0:1]
    stat_ref[...] = pack_stat(row, stat_ref.shape)


def weight_grad_kernel(dz, normed_ref, masked_ref, enc_ref, *refs):
    qgt_ref, kvt_ref, att_ref = refs[:3]
    outs, held = refs[3:-1], refs[-1]
    width = qgt_ref.shape[0]
    targets = [outs[0], outs[1], outs[2:-1], outs[-1]]

    def body(n, carry):
        place = dp_block(n, dz)
        held[:width] = nn(qgt_ref[...], normed_ref[place]).astype(BF)
        held[width : 3 * width] = nn(kvt_ref[...], enc_ref[place]).astype(BF)
        held[3 * width :] = nn(att_ref[...], masked_ref[place]).astype(BF)
        for k, target in enumerate(targets):

            @pl.when(n == k)
            def _():
                parts = target if isinstance(target, tuple) else (target,)
                first = 0
                for part in parts:
                    part[...] = held[first : first + part.shape[0]]
                    first += part.shape[0]

        return carry

    lax.fori_loop(0, 4, body, 0)


def partial_kernel(side, q_t_ref, kv_ref, at_t_ref, stat_ref, even, odd, out, kv_buf):
    width, tokens = q_t_ref.shape
    erows = kv_ref.shape[0] // NB
    a, b, c = mp_place()
    core = lax.rem(c + side, 2)
    for x in range(4):
        for z in range(2):
            out[z, x, 3 * tokens :, :] = stat_ref[...]
            owner = lax.rem(a + z, 2) * 8 + lax.bitwise_xor(b, x) * 2 + core
            start = pl.multiple_of(owner * erows, erows)
            line = (x * 2 + z) * erows
            kv_buf[line : line + erows, :] = kv_ref[pl.ds(start, erows), :]

    def block_of(n, shifts):
        return dp_block(lax.rem(n, 4), jnp.where(n < 4, shifts[0], shifts[1]))

    stacks = ((even, (0, 2)), (odd, (3, 1)))
    for stack, shifts in stacks:

        def enc_part(n, carry, stack=stack, shifts=shifts):
            line = pl.multiple_of(2 * tokens + block_of(n, shifts) * erows, erows)
            enc = nt(kv_buf[...], stack[n, :, width : 3 * width]).astype(BF)
            for x in range(4):
                for z in range(2):
                    first = (x * 2 + z) * erows
                    out[z, x, pl.ds(line, erows), :] = enc[first : first + erows]
            return carry

        lax.fori_loop(0, stack.shape[0], enc_part, 0, unroll=2)

    last = lax.rem(lax.axis_index("dp") + core, 2)
    for stack, shifts in stacks:

        @pl.when(last == shifts[0] % 2)
        def _():
            def parts(n, carry):
                place = block_of(n, shifts)
                xr = lax.bitwise_xor(lax.rem(lax.div(place, 2), 4), b)
                zr = lax.rem(lax.div(place, 8) + 2 - a, 2)
                out[zr, xr, :tokens, :] = nn(stack[n, :, :width], q_t_ref[...]).astype(BF)
                out_part = nn(stack[n, :, 3 * width :], at_t_ref[...]).astype(BF)
                out[zr, xr, tokens : 2 * tokens, :] = out_part
                return carry

            lax.fori_loop(0, stack.shape[0], parts, 0, unroll=2)


def add_rows(ins, out):
    rows, feat = out.shape[0] - EXTRA, out.shape[1]

    def body(step, carry):
        part = pl.ds(pl.multiple_of(step * CHUNK, CHUNK), CHUNK)
        total = ins[0][part, :].astype(F32)
        for ref in ins[1:]:
            total += ref[part, :].astype(F32)
        out[part, :] = total.astype(BF)
        return carry

    lax.fori_loop(0, rows // CHUNK, body, 0)
    stat = stat_of(ins[0][rows:])
    for ref in ins[1:]:
        stat += stat_of(ref[rows:])
    out[rows:] = pack_stat(stat, (EXTRA, feat))


def core_sum_kernel(keep_ref, got_ref, *outs):
    for z, out in enumerate(outs):

        def body(x, carry, z=z, out=out):
            add_rows([keep_ref.at[z, x], got_ref.at[z, x]], out.at[x])
            return carry

        lax.fori_loop(0, 4, body, 0)


def z_sum_kernel(keep_ref, got_ref, *outs):
    for n, out in enumerate(outs):

        def body(x, carry, n=n, out=out):
            add_rows([keep_ref.at[2 * n + x], got_ref.at[2 * n + x]], out.at[x])
            return carry

        lax.fori_loop(0, 2, body, 0)


def x_sum_kernel(first_ref, second_ref, *outs):
    for n, out in enumerate(outs):
        add_rows([first_ref.at[n], second_ref.at[n]], out)


def share_kernel(*refs):
    ins, outs = refs[:-4], refs[-4:]
    total = ins[0][...].astype(F32)
    for ref in ins[1:]:
        total += ref[...].astype(F32)
    total = total.astype(BF)
    width = outs[0].shape[1]
    for n, out in enumerate(outs[:3]):
        out[...] = total[n * width : (n + 1) * width].T
    outs[3][...] = total[3 * width :]


def last_kernel(len_ref, *refs):
    terms, (acts_ref, inv_ref, out_ref, in_ref, enc_ref) = refs[:2], refs[2:]
    tokens, feat = out_ref.shape[1:]
    rows = 3 * tokens
    total = [sum(ref[n * tokens : (n + 1) * tokens].astype(F32) for ref in terms) for n in range(3)]
    total[0], total[1] = total[0].T, total[1].T
    stat = sum(stat_of(ref[rows:]) for ref in terms)
    stat = jnp.broadcast_to(stat, (128, tokens)).T[:, :1] / (NB * feat)
    inv_rms = inv_ref[:, :1]
    dec = acts_ref[:tokens].astype(F32)
    out_ref[0] = (dec + total[1]).astype(BF)
    keep = lax.broadcasted_iota(jnp.int32, (tokens, feat), 0) < len_ref[0]
    masked = jnp.where(keep, acts_ref[tokens : 2 * tokens].astype(F32), 0.0)
    in_grad = masked + inv_rms * total[0] - dec * (inv_rms * inv_rms * stat)
    in_ref[0] = in_grad.astype(BF)
    erows = enc_ref.shape[1]
    for n in range(NB):
        enc_ref[0, :, n * feat : (n + 1) * feat] = total[2][n * erows : (n + 1) * erows].astype(BF)


def stack_pair(first, second):
    return call(pair_kernel, (first, second), [shape_of((2,) + first.shape)])[0]


def halves(first, second):
    half = shape_of((first.shape[0] // 2, first.shape[1]))
    return call(halves_kernel, (first, second), [half] * 2)


def gather(block, acts, begin):
    x3 = send_mp(acts, 0, 3, 0)
    before, behind = send_z(block, 1), send_z(block, -1)
    low, high = send_y(block, 1), send_y(block, -1)
    x3, to_x, again = after((x3, acts, block), low, high)
    x1, x2 = send_mp(to_x, 0, 1, 0), send_mp(to_x, 0, 2, 0)
    across = send_y(again, 2)

    x1, x2, x3, before, behind = after((x1, x2, x3, before, behind), across)
    (quad,) = call(quad_kernel, (acts, x1, x2, x3), [shape_of((4,) + acts.shape)])
    pair = stack_pair(before, behind)
    pair_low, pair_high = send_y(pair, 1), send_y(pair, -1)
    to_low, to_high = halves(before, behind)
    far_low, far_high = send_z(to_low, 1), send_z(to_high, -1)
    (to_other,) = after((quad,), far_low, far_high)
    other = send_mp(to_other, 1, 0, 0)

    pair_low, pair_high, far_low, far_high = after((pair_low, pair_high, far_low, far_high))
    (far,) = call(join_kernel, (far_low, far_high), [shape_of(block.shape)])
    f_low, f_high = send_y(far, 1), send_y(far, -1)
    to_low, to_high = call(pick_kernel, (pair_low, pair_high), [shape_of(block.shape)] * 2)
    across_b, across_a = send_y(to_low, 1), send_y(to_high, -1)

    quad, other, f_low, f_high = after((quad, other, f_low, f_high), across_a, across_b)
    (line,) = call(pair_kernel, (quad, other), [shape_of((2,) + quad.shape)])
    sibling = send_mp(line, 0, 0, 1)
    to_low, to_high = halves(f_low, f_high)
    last_low, last_high = send_y(to_low, 1), send_y(to_high, -1)
    return (
        (pair, pair_high, pair_low, across_b, across_a),
        (far, f_high, f_low, last_low, last_high),
        begin((line, sibling), (block, high, low, across)),
    )


CHUNK = 128


def summed(out, put, *terms):
    def body(step, carry):
        rows = pl.ds(pl.multiple_of(step * CHUNK, CHUNK), CHUNK)
        total = terms[0](rows).astype(F32)
        for term in terms[1:]:
            total += term(rows).astype(F32)
        put(out, rows, total.astype(BF))
        return carry

    lax.fori_loop(0, out.shape[-2] // CHUNK, body, 0)


def plain(ref):
    return lambda rows: ref[rows, :]


def of(ref, n):
    return lambda rows: ref[n, rows, :]


def put_plain(out, rows, value):
    out[rows, :] = value


def put_at(n):
    def put(out, rows, value):
        out[n, rows, :] = value

    return put


def far_kernel_sum(far1, far3, low, high, out1, out3):
    half = low.shape[0]
    for ref, part, out, first in ((far1, low, out1, 0), (far3, high, out3, half)):
        rest = slice(half - first, 2 * half - first)
        out[rest] = ref[rest]
        here = ref.at[first : first + half]
        summed(out.at[first : first + half], put_plain, plain(here), plain(part))


def second_sum_kernel(far0, far1, far3, bf1, bf2, bf3, bh1, bh2, bh3, up, down, far_low, far_high):
    summed(up, put_at(0), plain(bf1), plain(bf2))
    summed(up, put_at(1), plain(bh1))
    summed(down, put_at(0), plain(bf3))
    summed(down, put_at(1), plain(bh3), plain(bh2))
    half = far_low.shape[0]
    for out, first in ((far_low, 0), (far_high, half)):
        summed(out, put_plain, *(plain(ref.at[first : first + half]) for ref in (far0, far1, far3)))


def third_sum_kernel(bf0, bh0, up, down, low, high, before, behind):
    half = low.shape[0]
    for out, ref, n, part, first in ((before, bf0, 0, low, 0), (behind, bh0, 1, high, half)):

        def body(step, carry, out=out, ref=ref, n=n, part=part, first=first):
            begin = pl.multiple_of(step * CHUNK, CHUNK)
            rows, here = pl.ds(begin + first, CHUNK), pl.ds(begin, CHUNK)
            rest = pl.ds(begin + half - first, CHUNK)
            total = ref[rows, :].astype(F32) + up[n, rows, :].astype(F32)
            total += down[n, rows, :].astype(F32) + part[here, :].astype(F32)
            out[rows, :] = total.astype(BF)
            total = ref[rest, :].astype(F32) + up[n, rest, :].astype(F32)
            total += down[n, rest, :].astype(F32)
            out[rest, :] = total.astype(BF)
            return carry

        lax.fori_loop(0, half // CHUNK, body, 0)


def scatter(grads, partials):
    send = partials(1)
    core = send_mp(send, 0, 0, 1)
    far0, far1, far2_low, far2_high, far3 = grads(2, (send,))
    full = shape_of(far0.shape)
    pair = shape_of((2,) + far0.shape)
    far2_low, far2_high = send_y(far2_low, 1), send_y(far2_high, -1)
    bf0, bf1, bf2, bf3 = grads(1, (far0,))
    bh0, bh1, bh2, bh3 = grads(3, (bf0,))
    keep = partials(0)

    core, keep, far2_low, far2_high, bf2, bh2 = after(
        (core, keep, far2_low, far2_high, bf2, bh2)
    )
    own0, own1, own2, own3 = grads(0, (core,))
    part = shape_of(keep.shape[1:])
    own_z, other_z = call(core_sum_kernel, (keep, core), [part] * 2, moved=9 * MIB)
    other_z = send_mp(other_z, 1, 0, 0)
    bf2, bh2 = send_y(bf2, 1), send_y(bh2, -1)
    far1, far3 = call(far_kernel_sum, (far1, far3, far2_low, far2_high), [full] * 2)
    far1, far3 = send_y(far1, 1), send_y(far3, -1)

    far1, far3, bf2, bh2 = after((far1, far3, bf2, bh2))
    half = shape_of(far2_low.shape)
    up, down, far_low, far_high = call(
        second_sum_kernel, (far0, far1, far3, bf1, bf2, bf3, bh1, bh2, bh3),
        [pair, pair, half, half],
    )
    up, down = send_y(up, 1), send_y(down, -1)
    far_low, far_high = send_z(far_low, 1), send_z(far_high, -1)
    (other_z,) = after((other_z,), far_low, far_high)
    part = shape_of((2,) + keep.shape[2:])
    near_x, far_x = call(z_sum_kernel, (own_z, other_z), [part] * 2, moved=6 * MIB)
    far_x = send_x(far_x, 2)

    up, down, far_low, far_high, own1, own2, own3 = after(
        (up, down, far_low, far_high, own1, own2, own3)
    )
    before, behind = call(
        third_sum_kernel, (bf0, bh0, up, down, far_low, far_high), [full] * 2
    )
    own1, own3, before, behind = after((own1, own3, before, behind))
    before, behind = send_z(before, 1), send_z(behind, -1)
    own1, own3 = send_y(own1, 1), send_y(own3, -1)
    own2, own1 = after((own2, own1))
    own2 = send_y(own2, 2)
    part = shape_of(keep.shape[2:])
    own_x, next_x = call(x_sum_kernel, (near_x, far_x), [part] * 2, moved=3 * MIB)
    return (own0, own1, own2, own3, before, behind), (own_x, send_x(next_x, 1))


def local(
    dec_input,
    enc_output,
    query_weight,
    key_weight,
    value_weight,
    output_weight,
    cotangent,
    enc_lengths,
    dec_lengths,
):
    tokens, feat = dec_input.shape[1:]
    width = query_weight.shape[1]
    erows = enc_output.shape[1]
    keys = erows * NB
    scale = width ** (-0.5)
    unit = 2 * tokens * feat * width

    hbm = pl.BlockSpec(memory_space=pltpu.HBM)
    vmem = pl.BlockSpec(memory_space=pltpu.VMEM)
    weights, acts = pl.pallas_call(
        assemble_kernel,
        in_specs=[hbm] * 7,
        out_specs=[vmem] * 2,
        out_shape=[shape_of((feat, 4 * width)), shape_of((2 * tokens + keys, feat))],
        scratch_shapes=[
            pltpu.VMEM((width, feat), BF), pltpu.VMEM((erows, NB * feat), BF),
            pltpu.SemaphoreType.DMA((7,)),
        ],
        compiler_params=pltpu.CompilerParams(vmem_limit_bytes=56 * MIB),
    )(query_weight, key_weight, value_weight, output_weight, dec_input, cotangent, enc_output)
    acc_shape = shape_of((4, tokens, width), F32)
    stack_shape = shape_of((8, feat, 4 * width))

    def begin(pieces, own_group):
        normed, masked, encoded, inv_rms = call(
            prepare_kernel, pieces,
            [
                shape_of((NB, tokens, feat)), shape_of((NB, tokens, feat)),
                shape_of((NB, keys, feat)), shape_of((tokens, 128), F32),
            ],
            (dec_lengths,), moved=12 * MIB,
        )
        acc, own_stack = call(
            own_kernel, (normed, masked, encoded, *own_group), [acc_shape, stack_shape],
            flops=16 * unit, moved=4 * MIB,
        )
        return normed, masked, encoded, inv_rms, own_stack, acc

    near_group, far_group, start = gather(weights, acts, begin)
    normed, masked, encoded, inv_rms, own_stack, acc = start
    stacked = (normed, masked, encoded)
    acc, near_stack = call(
        near_kernel, (*stacked, *near_group, acc), [acc_shape, stack_shape],
        flops=32 * unit, moved=8 * MIB,
    )
    kshape = shape_of((keys, 2 * width))
    kv_grad, q_t, kv_t, at_t, stat, even_stack = call(
        functools.partial(far_kernel, scale), (*stacked, *far_group, acc, own_stack),
        [
            kshape, shape_of((width, tokens)), shape_of((2 * width, keys)),
            shape_of((width, tokens)), shape_of((EXTRA, tokens)), stack_shape,
        ],
        (enc_lengths,), flops=24 * unit, moved=4 * MIB, aliases=((10, 5),),
    )

    def grads(dz, others):
        (normed_in,) = after((normed,), *others) if others else (normed,)
        full, part = shape_of((4 * width, feat)), shape_of((2 * width, feat))
        outs = [full, full, part, part, full] if dz == 2 else [full] * 4
        return call(
            functools.partial(weight_grad_kernel, dz), (normed_in, masked, encoded, q_t, kv_t, at_t),
            outs, scratch=[pltpu.VMEM((4 * width, feat), BF)], flops=16 * unit, moved=4 * MIB,
        )

    def partials(side):
        out = shape_of((2, 4, 3 * tokens + EXTRA, feat))
        return call(
            functools.partial(partial_kernel, side),
            (q_t, kv_grad, at_t, stat, even_stack, near_stack),
            [out], scratch=[pltpu.VMEM((keys // 2, 2 * width), BF)], flops=32 * unit, moved=14 * MIB,
        )[0]

    shares, terms = scatter(grads, partials)
    query_grad, key_grad, value_grad, output_grad = call_out(
        share_kernel, shares, [shape_of((feat, width))] * 4
    )
    stack = shape_of((1, tokens, feat))
    layer_out, input_grad, enc_grad = call_out(
        last_kernel, (*terms, acts, inv_rms),
        [stack, stack, shape_of((1, erows, NB * feat))], (dec_lengths,),
    )
    return (layer_out, input_grad, enc_grad, query_grad, key_grad, value_grad, output_grad)


def solution(mesh):
    in_specs = (
        P("dp", None, "mp"),
        P("dp", "mp", None),
        P("dp", "mp"),
        P("dp", "mp"),
        P("dp", "mp"),
        P("mp", "dp"),
        P("dp", None, "mp"),
        P("dp"),
        P("dp"),
    )
    out_specs = (
        P("dp", None, "mp"),
        P("dp", None, "mp"),
        P("dp", "mp", None),
        P("dp", "mp"),
        P("dp", "mp"),
        P("dp", "mp"),
        P("mp", "dp"),
    )
    return jax.shard_map(local, mesh=mesh, in_specs=in_specs, out_specs=out_specs, check_vma=False)
```
